128 devices in a mesh: seq: 16 (over y_lo, z, core), kvh: 8 (over y_hi, x).
Axes of the slice: x: 4, y: 4 (y_hi: 2, y_lo: 2; y = y_hi * 2 + y_lo), z: 4, core: 2. Of those that a mesh axis runs over, the one named last changes fastest.
Arguments:
- hidden_in: bfloat16 [8192, 8192], P('seq', 'kvh'), may hold values from -10 to 10
- queries: bfloat16 [8192, 4096], P('seq', 'kvh'), may hold values from -8 to 8
- keys: bfloat16 [8192, 1024], P('seq', 'kvh'), may hold values from -12 to 12
- values: bfloat16 [8192, 1024], P('seq', 'kvh'), may hold values from -12 to 12
- out_weight: bfloat16 [4096, 8192], P('kvh'), may hold values from -0.09375 to 0.09375
- norm_gain: float32 [8192], replicated, may hold values from 0.1 to 1.9
- head_weight: bfloat16 [81920, 8192], P(('seq', 'kvh')), may hold values from -5 to 5
- caption_pos: int32 [256], replicated, may hold values from 0 to 8191, as said below
- targets: int32 [256], replicated, may hold values from 0 to 81919
Outputs:
- layer_out: bfloat16 [8192, 8192], P('seq', 'kvh')
- log_probs: float32 [256], replicated
The draws below stay inside these ranges and needn't reach their ends.
Inputs may be any that keep to these rules, and one draw needn't show every extreme that they name: `caption_pos`: positions increase; exactly one lies in each aligned run of 32 positions; the first is 0 and the last is 8191.
All inputs are finite; a program needn't handle non-finite values.
Results may differ from the reference program's by a relative error of at most 0.015.
Values may be sent and summed in bfloat16 or wider, within the bound.
A program may use at most 128 MiB of HBM per device.

```python
import math
import jax
import jax.numpy as jnp
from jax import lax

D = 8192
HD = 128
QPK = 4
TOK_DEV = 512
CAP = 256
KVH = 8
HQ = 32
L = 8192
VOCAB = 81920


def caption_positions(key):
    stride = L // CAP
    offsets = jax.random.randint(jax.random.fold_in(key, 901), (CAP,), 0, stride)
    offsets = offsets.at[0].set(0).at[CAP - 1].set(stride - 1)
    return (jnp.arange(CAP, dtype=jnp.int32) * stride + offsets).astype(jnp.int32)


def draw_caption_pos(key, part):
    return caption_positions(key)


def draw_targets(key, part):
    key = jax.random.fold_in(key, 31)
    seq_count = L // TOK_DEV
    span = VOCAB // seq_count
    per_owner = CAP // seq_count
    rows = jnp.arange(CAP, dtype=jnp.int32)
    owner = rows // per_owner
    nearby = (owner + 1) % seq_count * span + jax.random.randint(jax.random.fold_in(key, 1), (CAP,), 0, span)
    anywhere = jax.random.randint(jax.random.fold_in(key, 2), (CAP,), 0, VOCAB)
    return jnp.where(rows % 2 == 0, nearby, anywhere).astype(jnp.int32)


def draw_hidden_in(key, part):
    key = jax.random.fold_in(key, 21)
    drawn = 0.5 * jnp.clip(jax.random.normal(key, (L, D), jnp.float32), -5.0, 5.0)
    return drawn.astype(jnp.bfloat16)


def draw_queries(key, part):
    key = jax.random.fold_in(key, 22)
    drawn = jnp.clip(jax.random.normal(key, (L, HQ * HD), jnp.float32), -6.0, 6.0)
    return drawn.astype(jnp.bfloat16)


def draw_keys(key, part):
    key = jax.random.fold_in(key, 23)
    drawn = 2.0 * jnp.clip(jax.random.normal(key, (L, KVH * HD), jnp.float32), -6.0, 6.0)
    return drawn.astype(jnp.bfloat16)


def draw_head_weight(key, part):
    key = jax.random.fold_in(key, 24)
    spread = 3.0 / D ** 0.5
    drawn = spread * jnp.clip(jax.random.normal(key, (VOCAB, D), jnp.float32), -6.0, 6.0)
    return drawn.astype(jnp.bfloat16)


def steps_of(rng, extent, shards, smallest, top_value):
    loudness, own = 1.0, jax.random.fold_in(rng, 6)
    for dim, blocks in shards:
        heights = jnp.exp(jax.random.uniform(jax.random.fold_in(own, dim), (blocks,), jnp.float32, smallest / len(shards), top_value / len(shards)))
        loudness = loudness * jnp.repeat(heights, extent[dim] // blocks).reshape([-1 if axis == dim else 1 for axis in range(len(extent))])
    return loudness


def scatter_about(key, shape, scale, limit, shards=(), kind=jnp.bfloat16):
    factor_of = steps_of(key, shape, shards, -0.22, 0.18) if shards else 1.0
    values = jax.random.normal(key, shape, jnp.float32) * scale * factor_of
    return jnp.minimum(jnp.maximum(values, -limit), limit).astype(kind)


def setup_inputs(seed: int = 0) -> dict:
    streams_of = jax.random.split(jax.random.key(seed), 10)
    hidden_in = draw_hidden_in(jax.random.fold_in(streams_of[9], 71), 0)
    queries = draw_queries(jax.random.fold_in(streams_of[9], 71), 0)
    keys = draw_keys(jax.random.fold_in(streams_of[9], 71), 0)
    values = scatter_about(streams_of[3], (L, KVH * HD), 2.0, 12.0, ((0, 16), (1, 8)))
    out_weight = scatter_about(streams_of[4], (HQ * HD, D), (HQ * HD) ** -0.5, 0.09375, ((0, 8),))
    norm_gain = jnp.clip(1.0 + 0.18 * jax.random.normal(streams_of[5], (D,), jnp.float32), 0.1, 1.9)
    head_weight = draw_head_weight(jax.random.fold_in(streams_of[9], 71), 0)
    caption_pos = draw_caption_pos(jax.random.fold_in(streams_of[9], 71), 0)
    targets = draw_targets(jax.random.fold_in(streams_of[9], 71), 0)
    return dict(hidden_in=hidden_in, queries=queries, keys=keys, values=values, out_weight=out_weight, norm_gain=norm_gain, head_weight=head_weight, caption_pos=caption_pos, targets=targets)


def reference(hidden_in, queries, keys, values, out_weight, norm_gain, head_weight, caption_pos, targets):
    block_rows = math.gcd(L, 1024)
    score_scale = HD ** (-0.5)
    attended_blocks = []
    for first_row in range(0, L, block_rows):
        stop_row = first_row + block_rows
        query_position = jnp.arange(first_row, stop_row)
        key_position = jnp.arange(stop_row)
        allowed = key_position[None, :] <= query_position[:, None]
        head_outputs = []
        for head_group in range(KVH):
            query_group = queries[first_row:stop_row, head_group * QPK * HD:(head_group + 1) * QPK * HD]
            query_group = query_group.astype(jnp.float32).reshape(block_rows, QPK, HD)
            key_group = keys[:stop_row, head_group * HD:(head_group + 1) * HD].astype(jnp.float32)
            value_group = values[:stop_row, head_group * HD:(head_group + 1) * HD].astype(jnp.float32)
            scores = jnp.einsum('rhd,kd->hrk', query_group, key_group) * score_scale
            scores = jnp.where(allowed[None], scores, -1e+30)
            weights = jnp.exp(scores - lax.optimization_barrier(jnp.max(scores, axis=2, keepdims=True)))
            totals = lax.optimization_barrier(jnp.sum(weights, axis=2))
            weights_low = lax.optimization_barrier(weights.astype(jnp.bfloat16))
            mixed = jnp.einsum('hrk,kd->hrd', weights_low.astype(jnp.float32), value_group)
            mixed = mixed / totals[:, :, None]
            mixed = jnp.transpose(mixed, (1, 0, 2)).reshape(block_rows, QPK * HD)
            head_outputs.append(mixed.astype(jnp.bfloat16))
        attended_blocks.append(jnp.concatenate(head_outputs, axis=1))
    attended = jnp.concatenate(attended_blocks, axis=0)
    layer_sum = jnp.zeros((L, D), jnp.float32)
    for head_group in range(KVH):
        columns = slice(head_group * QPK * HD, (head_group + 1) * QPK * HD)
        partial_term = jnp.dot(attended[:, columns], out_weight[columns, :], preferred_element_type=jnp.float32)
        partial_low = lax.optimization_barrier(partial_term.astype(jnp.bfloat16))
        layer_sum = layer_sum + partial_low.astype(jnp.float32)
    layer_out = (hidden_in.astype(jnp.float32) + layer_sum).astype(jnp.bfloat16)
    caption_rows = jnp.take(layer_out, caption_pos, axis=0).astype(jnp.float32)
    mean_square = lax.optimization_barrier(jnp.mean(caption_rows * caption_rows, axis=1, keepdims=True))
    normed = (caption_rows * lax.rsqrt(mean_square + 1e-06) * norm_gain.astype(jnp.float32)[None, :]).astype(jnp.bfloat16)
    logits = jnp.dot(normed, head_weight.T, preferred_element_type=jnp.float32)
    row_max = lax.optimization_barrier(jnp.max(logits, axis=1))
    log_total = row_max + jnp.log(lax.optimization_barrier(jnp.sum(jnp.exp(logits - row_max[:, None]), axis=1)))
    picked = jnp.take_along_axis(logits, targets[:, None].astype(jnp.int32), axis=1)[:, 0]
    log_probs = picked - log_total
    return (layer_out, log_probs)
```

```python
import functools
import jax
import jax.numpy as jnp
from jax import lax
from jax.experimental import pallas as pl
from jax.experimental.pallas import tpu as pltpu
from jax.sharding import PartitionSpec as P

MESH = pl.DeviceIdType.MESH
F32 = jnp.float32
BF16 = jnp.bfloat16
NT = (((1,), (1,)), ((), ()))
NEG = -1e30
SEQ = 16
KVH = 8
PAIRS = 8
XS = 4
TOK = 512
HD = 128
HEADS = 4
RB = 128
NRB = TOK // RB
CAPS = 16
NCAP = SEQ * CAPS
FEAT = 1024
VOC = 640
SCALE = HD ** (-0.5)
SCALE2 = SCALE * 1.4426950408889634


def rcopy(src, dst, send_sem, recv_sem, device):
    return pltpu.make_async_remote_copy(
        src_ref=src,
        dst_ref=dst,
        send_sem=send_sem,
        recv_sem=recv_sem,
        device_id=device,
        device_id_type=MESH,
    )


def kernel(
    q_ref, k_ref, v_ref, hid_ref, ow_ref, gain_ref, hw_ref, cap_ref, tgt_ref,
    out_ref, lp_ref,
    kv, m_s, acc_s, wbuf, hw, call, ncap, abuf, psend, precv, lacc,
    cq, cpo, cpi, cro, cri, logit, stat, st1, st2,
    wl_m, wo_m, hw_m, kv_s, kv_r, kf_s, kf_r, w_s, w_r, wf_s, wf_r,
    cq_s, cq_r, cp_s, cp_r, cr_s, cr_r, ck_s, ck_r, cs_s, cs_r, cf_s, cf_r,
    a_s, a_r, y_s, y_r, s1_s, s1_r, s2_s, s2_r,
):
    s = lax.axis_index("seq")
    k = lax.axis_index("kvh")
    pair, core = lax.div(s, 2), lax.rem(s, 2)
    yhi, x = lax.div(k, XS), lax.rem(k, XS)
    other_y = 1 - yhi
    sib = (2 * pair + 1 - core, k)
    y_dev = (s, other_y * XS + x)

    def pair_dev(p):
        return (2 * p + core, k)

    def x_dev(xx):
        return (s, yhi * XS + xx)

    def cols(kk):
        return pl.ds(pl.multiple_of(kk * FEAT, FEAT), FEAT)

    half = pl.ds(pl.multiple_of(core * TOK, TOK), TOK)
    whalf = pl.ds(pl.multiple_of(core * 256, 256), 256)

    own_w = [
        pltpu.make_async_copy(ow_ref.at[:, cols(y * XS + x)], wbuf.at[y, x], wo_m.at[y])
        for y in range(2)
    ]
    local_w = [
        pltpu.make_async_copy(ow_ref.at[:, cols(i)], hw.at[0:TOK, cols(i)], wl_m.at[i])
        for i in range(KVH)
    ]
    head_copy = pltpu.make_async_copy(hw_ref, hw, hw_m.at[0])
    barrier = pltpu.get_barrier_semaphore()
    for j in range(1, SEQ):
        pl.semaphore_signal(barrier, inc=1, device_id=(lax.rem(s + j, SEQ), k), device_id_type=MESH)
    for j in range(1, KVH):
        pl.semaphore_signal(barrier, inc=1, device_id=(s, lax.rem(k + j, KVH)), device_id_type=MESH)
    for c in local_w + own_w:
        c.start()
    kv[pair, half, 0:HD] = k_ref[...]
    kv[pair, half, HD : 2 * HD] = v_ref[...]
    own_rows = pl.ds(pl.multiple_of(s * 64, 64), CAPS)
    spots = cap_ref[own_rows, :] - s * TOK
    sel = (lax.broadcasted_iota(jnp.int32, (CAPS, TOK), 1) == spots).astype(F32).astype(BF16)
    for h in range(HEADS):
        picked = jnp.dot(sel, q_ref[:, h * HD : (h + 1) * HD], preferred_element_type=F32)
        cq[s, h * CAPS : (h + 1) * CAPS, :] = picked.astype(BF16)
    pl.semaphore_wait(barrier, SEQ - 1 + KVH - 1)

    def cq_copy(j):
        return rcopy(cq.at[s], cq.at[s], cq_s.at[j], cq_r.at[s], (j, k))

    def start_cq(j, carry):
        cq_copy(j).start()
        return carry

    lax.fori_loop(0, s, start_cq, 0)

    def kv_copy(j):
        block = kv.at[pair, half]
        return rcopy(block, block, kv_s.at[j], kv_r.at[pair], pair_dev(pair + j))

    def kf_copy(p):
        block = kv.at[p, half]
        return rcopy(block, block, kf_s.at[p], kf_r.at[p], sib)

    kf_copy(pair).start()
    for j in range(1, PAIRS):
        pl.when(pair + j < PAIRS)(lambda j=j: kv_copy(j).start())

    def w_copy(j, y):
        xx = lax.rem(x + j, XS)
        return rcopy(
            ow_ref.at[whalf, cols(y * XS + xx)], wbuf.at[y, x, whalf], w_s.at[y, j], w_r.at[y, x], x_dev(xx)
        )

    for j in range(1, XS):
        for y in range(2):
            w_copy(j, y).start()

    ones = jnp.ones((2 * TOK, HD), BF16)

    def attend(rb, p, own):
        rows = pl.ds(pl.multiple_of(rb * RB, RB), RB)
        keys = kv[p, :, 0:HD]
        vals = jnp.concatenate([kv[p, :, HD : 2 * HD], ones], axis=1)
        if own:
            row_at = lax.broadcasted_iota(jnp.int32, (RB, 2 * TOK), 0) + (core * TOK + rb * RB)
            allowed = lax.broadcasted_iota(jnp.int32, (RB, 2 * TOK), 1) <= row_at
        for h in range(HEADS):
            at = rb * HEADS + h
            query = q_ref[rows, h * HD : (h + 1) * HD]
            sc = lax.dot_general(query, keys, NT, preferred_element_type=F32)
            if own:
                sc = jnp.where(allowed, sc, NEG)
                top = jnp.broadcast_to(jnp.max(sc, axis=1, keepdims=True), (RB, HD))
            else:
                old = m_s[at]
                top = jnp.maximum(old, jnp.max(sc, axis=1, keepdims=True))
            w = jnp.exp2((sc - top[:, 0:1]) * SCALE2).astype(BF16)
            m_s[at] = top
            pv = jnp.dot(w, vals, preferred_element_type=F32)
            if own:
                acc_s[at] = pv
            else:
                f = jnp.exp2((old - top) * SCALE2)
                acc_s[at] = acc_s[at] * jnp.concatenate([f, f], axis=1) + pv

    def attend_all(p, own):
        def step(rb, carry):
            attend(rb, p, own)
            return carry

        lax.fori_loop(0, NRB, step, 0)

    def half_arrived(j):
        p = pair - j
        block = kv.at[p, half]
        rcopy(block, block, kv_s.at[0], kv_r.at[p], sib).wait_recv()
        kf_copy(p).start()

    def sib_arrived(p):
        block = kv.at[p, half]
        rcopy(block, block, kf_s.at[p], kf_r.at[p], sib).wait_recv()

    sib_arrived(pair)
    attend_all(pair, True)
    pl.when(pair >= 1)(lambda: half_arrived(1))

    def wait_cq(j, carry):
        rcopy(cq.at[j], cq.at[j], cq_s.at[j], cq_r.at[j], sib).wait_recv()
        return carry

    lax.fori_loop(s + 1, SEQ, wait_cq, 0)
    own_vals = jnp.concatenate([v_ref[...], jnp.ones((TOK, HD), BF16)], axis=1)
    lane = lax.broadcasted_iota(jnp.int32, (TOK, HD), 1)
    for g in range(2):
        queries = cq[g * 8 : (g + 1) * 8].reshape(TOK, HD)
        sc = lax.dot_general(queries, k_ref[...], NT, preferred_element_type=F32)
        key_at = lax.broadcasted_iota(jnp.int32, (TOK, TOK), 1) + s * TOK
        sc = jnp.where(key_at <= cap_ref[g * TOK : (g + 1) * TOK, :], sc, NEG)
        top = jnp.broadcast_to(jnp.max(sc, axis=1, keepdims=True), (TOK, HD))
        w = jnp.exp2((sc - top[:, 0:1]) * SCALE2).astype(BF16)
        pv = jnp.dot(w, own_vals, preferred_element_type=F32)
        total = pv[:, HD:]
        lse = top * SCALE + jnp.log(total)
        hi = lse.astype(BF16).astype(F32)
        mid = (lse - hi).astype(BF16).astype(F32)
        low = lse - hi - mid
        parts = jnp.where(lane < 32, hi, jnp.where(lane < 64, mid, low))
        both = jnp.concatenate([pv[:, :HD] / total, parts], axis=1).astype(BF16)
        cpo[g * 8 : (g + 1) * 8] = both.reshape(8, 64, 2 * HD)

    def cp_copy(j):
        return rcopy(cpo.at[j], cpi.at[s], cp_s.at[j], cp_r.at[s], (j, k))

    def start_cp(j, carry):
        cp_copy(j).start()
        return carry

    lax.fori_loop(s + 1, SEQ, start_cp, 0)

    def phase_one(j):
        pl.when(pair >= j + 1)(lambda: half_arrived(j + 1))

        def work():
            sib_arrived(pair - j)
            attend_all(pair - j, False)

        pl.when(pair >= j)(work)

    phase_one(1)

    def unpack(block):
        t = block[:, HD:].astype(F32)
        return block[:, :HD].astype(F32), t[:, 0:1] + t[:, 32:33] + t[:, 64:65]

    def combine(j, carry):
        top, total, acc = carry
        rcopy(cpi.at[j], cpi.at[j], cp_s.at[j], cp_r.at[j], sib).wait_recv()
        o, lse = unpack(cpi[j])
        new = jnp.maximum(top, lse)
        a, b = jnp.exp(top - new), jnp.exp(lse - new)
        return new, total * a + b, acc * a + o * b

    own_o, own_lse = unpack(cpo[s])
    top, total, acc = lax.fori_loop(0, s, combine, (own_lse, jnp.ones((64, 1), F32), own_o))
    att = acc / total
    att = jnp.concatenate([att[h * CAPS : (h + 1) * CAPS] for h in range(HEADS)], axis=1).astype(BF16)
    for i in range(KVH):
        local_w[i].wait()
        cro[i] = jnp.dot(att, hw[0:TOK, i * FEAT : (i + 1) * FEAT], preferred_element_type=F32).astype(BF16)

    def cr_copy(j):
        kk = lax.rem(k + j, KVH)
        return rcopy(cro.at[kk], cri.at[k], cr_s.at[j], cr_r.at[k], (s, kk))

    for j in range(1, KVH):
        cr_copy(j).start()
    head_copy.start()

    phase_one(2)

    cap_sum = cro[k].astype(F32) + jnp.dot(sel, hid_ref[...], preferred_element_type=F32)
    for j in range(1, KVH):
        kk = lax.rem(k + j, KVH)
        rcopy(cri.at[kk], cri.at[kk], cr_s.at[0], cr_r.at[kk], sib).wait_recv()
        cap_sum = cap_sum + cri[kk].astype(F32)

    def cap_rows(ss):
        return pl.ds(pl.multiple_of(ss * CAPS, CAPS), CAPS)

    call[k, cap_rows(s), :] = cap_sum.astype(BF16)

    def ck_copy(j):
        block = call.at[k, cap_rows(s)]
        return rcopy(block, block, ck_s.at[j], ck_r.at[k], (s, lax.rem(k + j, KVH)))

    for j in range(1, KVH):
        ck_copy(j).start()

    phase_one(3)

    for j in range(1, KVH):
        kk = lax.rem(k + j, KVH)
        block = call.at[kk, cap_rows(s)]
        rcopy(block, block, ck_s.at[0], ck_r.at[kk], sib).wait_recv()

    def cs_copy(j):
        block = call.at[:, cap_rows(s)]
        return rcopy(block, block, cs_s.at[j], cs_r.at[pair], pair_dev(lax.rem(pair + j, PAIRS)))

    def cf_copy(p):
        block = call.at[:, cap_rows(2 * p + core)]
        return rcopy(block, block, cf_s.at[p], cf_r.at[p], sib)

    cf_copy(pair).start()
    for j in range(1, PAIRS):
        cs_copy(j).start()

    for j in range(4, PAIRS):
        if j + 1 < PAIRS:
            pl.when(pair >= j + 1)(lambda j=j: half_arrived(j + 1))
        pl.when(pair >= j)(lambda j=j: sib_arrived(pair - j))

    def a_copy(rb, j):
        block = abuf.at[rb, x]
        return rcopy(block, block, a_s.at[rb, j], a_r.at[rb, x], x_dev(lax.rem(x + j, XS)))

    def finish(rb):
        def step(j, carry):
            attend(rb, pair - j, False)
            return carry

        lax.fori_loop(4, pair + 1, step, 0)
        for h in range(HEADS):
            done = acc_s[rb * HEADS + h]
            abuf[rb, x, :, h * HD : (h + 1) * HD] = (done[:, :HD] / done[:, HD:]).astype(BF16)
        for j in range(1, XS):
            a_copy(rb, j).start()

    def y_copy(rb):
        return rcopy(psend.at[rb], precv.at[rb], y_s.at[rb], y_r.at[rb], y_dev)

    def project(rb):
        for j in range(1, XS):
            xx = lax.rem(x + j, XS)
            block = abuf.at[rb, xx]
            rcopy(block, block, a_s.at[rb, 0], a_r.at[rb, xx], sib).wait_recv()

        def product(y):
            parts = [jnp.dot(abuf[rb, xx], wbuf[y, xx], preferred_element_type=F32) for xx in range(XS)]
            return (parts[0] + parts[1]) + (parts[2] + parts[3])

        psend[rb] = product(other_y).astype(BF16)
        y_copy(rb).start()
        lacc[rb] = product(yhi) + hid_ref[rb * RB : (rb + 1) * RB, :].astype(F32)

    def w_arrived():
        for c in own_w:
            c.wait()
        for j in range(1, XS):
            xx = lax.rem(x + j, XS)
            for y in range(2):
                block = wbuf.at[y, xx, whalf]
                rcopy(block, block, w_s.at[y, 0], w_r.at[y, xx], sib).wait_recv()
                wf_copy(j, y).start()
        for j in range(1, XS):
            xx = lax.rem(x + j, XS)
            for y in range(2):
                block = wbuf.at[y, xx, whalf]
                rcopy(block, block, wf_s.at[y, xx], wf_r.at[y, xx], sib).wait_recv()

    def wf_copy(j, y):
        xx = lax.rem(x + j, XS)
        block = wbuf.at[y, xx, whalf]
        return rcopy(block, block, wf_s.at[y, xx], wf_r.at[y, xx], sib)

    finish(0)
    finish(1)
    w_arrived()
    project(0)
    finish(2)
    project(1)
    finish(3)
    project(2)
    project(3)

    for j in range(1, PAIRS):
        p = lax.rem(pair + PAIRS - j, PAIRS)
        block = call.at[:, cap_rows(2 * p + core)]
        rcopy(block, block, cs_s.at[0], cs_r.at[p], sib).wait_recv()
        cf_copy(p).start()

    def final(rb):
        rcopy(psend.at[rb], precv.at[rb], y_s.at[rb], y_r.at[rb], sib).wait_recv()
        out_ref[rb * RB : (rb + 1) * RB, :] = (lacc[rb] + precv[rb].astype(F32)).astype(BF16)

    for rb in range(NRB):
        final(rb)
    for p in range(PAIRS):
        block = call.at[:, cap_rows(2 * p + core)]
        rcopy(block, block, cf_s.at[p], cf_r.at[p], sib).wait_recv()
    head_copy.wait()

    def normalise(i, carry):
        rows = pl.ds(pl.multiple_of(i * 32, 32), 32)
        wide = [call[kk, rows, :].astype(F32) for kk in range(KVH)]
        squares = functools.reduce(lambda a, b: a + b, [t * t for t in wide])
        mean = jnp.sum(squares, axis=1, keepdims=True) * (1.0 / (KVH * FEAT))
        r = lax.rsqrt(mean + 1e-06)
        for kk in range(KVH):
            ncap[kk, rows, :] = (wide[kk] * r * gain_ref[kk : kk + 1, :]).astype(BF16)
        return carry

    lax.fori_loop(0, NCAP // 32, normalise, 0)
    logit[...] = jnp.zeros((VOC, NCAP), F32)

    def logit_step(kk, carry):
        logit[...] += lax.dot_general(hw[:, cols(kk)], ncap[kk], NT, preferred_element_type=F32)
        return carry

    lax.fori_loop(0, KVH, logit_step, 0)
    lt = logit[...]
    ids = lax.broadcasted_iota(jnp.int32, (VOC, NCAP), 0) + (s * KVH + k) * VOC
    top = jnp.max(lt, axis=0, keepdims=True)
    st1[k, 0:1, :] = top
    st1[k, 1:2, :] = jnp.sum(jnp.exp(lt - top), axis=0, keepdims=True)
    st1[k, 2:3, :] = jnp.sum(jnp.where(ids == tgt_ref[...], lt, 0.0), axis=0, keepdims=True)

    def s1_copy(j):
        return rcopy(st1.at[k], st1.at[k], s1_s.at[j], s1_r.at[k], (s, lax.rem(k + j, KVH)))

    def s2_copy(j):
        return rcopy(st2.at[s], st2.at[s], s2_s.at[j], s2_r.at[s], (lax.rem(s + j, SEQ), k))

    def merge(blocks):
        top = jnp.max(blocks[:, 0, :], axis=0, keepdims=True)
        total = jnp.sum(blocks[:, 1, :] * jnp.exp(blocks[:, 0, :] - top), axis=0, keepdims=True)
        return top, total, jnp.sum(blocks[:, 2, :], axis=0, keepdims=True)

    for j in range(1, KVH):
        s1_copy(j).start()
    for j in range(1, KVH):
        kk = lax.rem(k + j, KVH)
        rcopy(st1.at[kk], st1.at[kk], s1_s.at[0], s1_r.at[kk], sib).wait_recv()
    top, total, target = merge(st1[...])
    st2[s, 0:1, :] = top
    st2[s, 1:2, :] = total
    st2[s, 2:3, :] = target
    for j in range(1, SEQ):
        s2_copy(j).start()
    for j in range(1, SEQ):
        ss = lax.rem(s + j, SEQ)
        rcopy(st2.at[ss], st2.at[ss], s2_s.at[0], s2_r.at[ss], sib).wait_recv()
    top, total, target = merge(st2[...])
    lp_ref[...] = target - (top + jnp.log(total))

    def wait_cq_sent(j, carry):
        cq_copy(j).wait_send()
        return carry

    def wait_cp_sent(j, carry):
        cp_copy(j).wait_send()
        return carry

    def wait_kf_sent(p, carry):
        kf_copy(p).wait_send()
        return carry

    lax.fori_loop(0, s, wait_cq_sent, 0)
    lax.fori_loop(s + 1, SEQ, wait_cp_sent, 0)
    lax.fori_loop(0, pair + 1, wait_kf_sent, 0)
    for j in range(1, PAIRS):
        pl.when(pair + j < PAIRS)(lambda j=j: kv_copy(j).wait_send())
        cs_copy(j).wait_send()
    for p in range(PAIRS):
        cf_copy(p).wait_send()
    for j in range(1, XS):
        for y in range(2):
            w_copy(j, y).wait_send()
            wf_copy(j, y).wait_send()
        for rb in range(NRB):
            a_copy(rb, j).wait_send()
    for rb in range(NRB):
        y_copy(rb).wait_send()
    for j in range(1, KVH):
        cr_copy(j).wait_send()
        ck_copy(j).wait_send()
        s1_copy(j).wait_send()
    for j in range(1, SEQ):
        s2_copy(j).wait_send()


def body(hidden_in, queries, keys, values, out_weight, norm_gain, head_weight, caption_pos, targets):
    cap_col = jnp.broadcast_to(caption_pos.reshape(SEQ, 1, CAPS), (SEQ, HEADS, CAPS)).reshape(SEQ * 64, 1)
    vmem = pl.BlockSpec(memory_space=pltpu.VMEM)
    hbm = pl.BlockSpec(memory_space=pl.ANY)
    dma = lambda *shape: pltpu.SemaphoreType.DMA(shape)
    layer_out, log_probs = pl.pallas_call(
        kernel,
        name="score_captions",
        out_shape=(
            jax.ShapeDtypeStruct((TOK, FEAT), BF16),
            jax.ShapeDtypeStruct((1, NCAP), F32),
        ),
        in_specs=[vmem, vmem, vmem, vmem, hbm, vmem, hbm, vmem, vmem],
        out_specs=(vmem, vmem),
        scratch_shapes=[
            pltpu.VMEM((PAIRS, 2 * TOK, 2 * HD), BF16),
            pltpu.VMEM((NRB * HEADS, RB, HD), F32),
            pltpu.VMEM((NRB * HEADS, RB, 2 * HD), F32),
            pltpu.VMEM((2, XS, TOK, FEAT), BF16),
            pltpu.VMEM((VOC, KVH * FEAT), BF16),
            pltpu.VMEM((KVH, NCAP, FEAT), BF16),
            pltpu.VMEM((KVH, NCAP, FEAT), BF16),
            pltpu.VMEM((NRB, XS, RB, HEADS * HD), BF16),
            pltpu.VMEM((NRB, RB, FEAT), BF16),
            pltpu.VMEM((NRB, RB, FEAT), BF16),
            pltpu.VMEM((NRB, RB, FEAT), F32),
            pltpu.VMEM((SEQ, 64, HD), BF16),
            pltpu.VMEM((SEQ, 64, 2 * HD), BF16),
            pltpu.VMEM((SEQ, 64, 2 * HD), BF16),
            pltpu.VMEM((KVH, CAPS, FEAT), BF16),
            pltpu.VMEM((KVH, CAPS, FEAT), BF16),
            pltpu.VMEM((VOC, NCAP), F32),
            pltpu.VMEM((8, NCAP), F32),
            pltpu.VMEM((KVH, 8, NCAP), F32),
            pltpu.VMEM((SEQ, 8, NCAP), F32),
            dma(KVH), dma(2), dma(1),
            dma(PAIRS), dma(PAIRS), dma(PAIRS), dma(PAIRS),
            dma(2, XS), dma(2, XS), dma(2, XS), dma(2, XS),
            dma(SEQ), dma(SEQ), dma(SEQ), dma(SEQ),
            dma(KVH), dma(KVH), dma(KVH), dma(KVH),
            dma(PAIRS), dma(PAIRS), dma(PAIRS), dma(PAIRS),
            dma(NRB, XS), dma(NRB, XS), dma(NRB), dma(NRB),
            dma(KVH), dma(KVH), dma(SEQ), dma(SEQ),
        ],
        compiler_params=pltpu.CompilerParams(
            collective_id=0, has_side_effects=True, vmem_limit_bytes=60 * 1024 * 1024
        ),
    )(
        queries, keys, values, hidden_in, out_weight, norm_gain.reshape(KVH, FEAT), head_weight,
        cap_col, targets.reshape(1, NCAP),
    )
    return layer_out, log_probs.reshape(NCAP)


def solution(mesh):
    in_specs = (
        P("seq", "kvh"),
        P("seq", "kvh"),
        P("seq", "kvh"),
        P("seq", "kvh"),
        P("kvh", None),
        P(),
        P(("seq", "kvh"), None),
        P(),
        P(),
    )
    out_specs = (P("seq", "kvh"), P())
    return jax.shard_map(body, mesh=mesh, in_specs=in_specs, out_specs=out_specs, check_vma=False)
```

```python
import functools
import jax
import jax.numpy as jnp
from jax import lax
from jax.experimental import pallas as pl
from jax.experimental.pallas import tpu as pltpu
from jax.sharding import PartitionSpec as P

MESH = pl.DeviceIdType.MESH
F32 = jnp.float32
BF16 = jnp.bfloat16
NT = (((1,), (1,)), ((), ()))
NEG = -1e30
SEQ = 16
KVH = 8
PAIRS = 8
XS = 4
TOK = 512
HD = 128
HEADS = 4
RB = 128
NRB = TOK // RB
CAPS = 16
NCAP = SEQ * CAPS
FEAT = 1024
VOC = 640
SCALE = HD ** (-0.5)
SCALE2 = SCALE * 1.4426950408889634


def rcopy(src, dst, send_sem, recv_sem, device):
    return pltpu.make_async_remote_copy(
        src_ref=src,
        dst_ref=dst,
        send_sem=send_sem,
        recv_sem=recv_sem,
        device_id=device,
        device_id_type=MESH,
    )


def kernel(
    q_ref, k_ref, v_ref, hid_ref, ow_ref, gain_ref, hw_ref, pos_ref, tgt_ref,
    out_ref, lp_ref,
    kv, m_s, acc_s, wbuf, hw, call, ncap, abuf, psend, precv, lacc,
    cap_ref, cq, cpo, cpi, cro, cri, ssq, logit, st1, st2,
    wl_m, wo_m, hw_m, kv_s, kv_r, kf_s, kf_r, kz_s, w_s, w_r, wf_s, wf_r,
    v_s, v_r, vf_s, vf_r, vy_s, vy_r,
    cq_s, cq_r, cp_s, cp_r, cr_s, cr_r, ck_s, ck_r, cy_s, cy_r, cs_s, cs_r, cf_s, cf_r,
    a_s, a_r, y_s, y_r, s1_s, s1_r, s2_s, s2_r,
):
    s = lax.axis_index("seq")
    k = lax.axis_index("kvh")
    pair, core = lax.div(s, 2), lax.rem(s, 2)
    ylo, z = lax.div(pair, 4), lax.rem(pair, 4)
    yhi, x = lax.div(k, XS), lax.rem(k, XS)
    other_y = 1 - yhi
    sib = (2 * pair + 1 - core, k)
    y_dev = (s, other_y * XS + x)

    def pair_dev(p):
        return (2 * p + core, k)

    def x_dev(xx):
        return (s, yhi * XS + xx)

    def cols(kk):
        return pl.ds(pl.multiple_of(kk * FEAT, FEAT), FEAT)

    half = pl.ds(pl.multiple_of(core * TOK, TOK), TOK)
    whalf = pl.ds(pl.multiple_of(core * 256, 256), 256)
    y_pair = (1 - ylo) * 4 + z

    def quarter(yy):
        return pl.ds(pl.multiple_of((yy * 2 + core) * 128, 128), 128)


    own_w = [
        pltpu.make_async_copy(ow_ref.at[:, cols(y * XS + x)], wbuf.at[y, x], wo_m.at[y])
        for y in range(2)
    ]
    local_w = [
        pltpu.make_async_copy(ow_ref.at[:, cols(i)], hw.at[0:TOK, cols(i)], wl_m.at[i])
        for i in range(KVH)
    ]
    head_copy = pltpu.make_async_copy(hw_ref, hw, hw_m.at[0])
    barrier = pltpu.get_barrier_semaphore()
    for j in range(1, SEQ):
        pl.semaphore_signal(barrier, inc=1, device_id=(lax.rem(s + j, SEQ), k), device_id_type=MESH)
    for j in range(1, KVH):
        pl.semaphore_signal(barrier, inc=1, device_id=(s, lax.rem(k + j, KVH)), device_id_type=MESH)
    for j in range(1, KVH):
        pl.semaphore_signal(
            barrier, inc=1, device_id=(2 * y_pair + core, lax.rem(k + j, KVH)), device_id_type=MESH
        )
    for c in local_w + own_w:
        c.start()
    kv[pair, half, 0:HD] = k_ref[...]
    kv[pair, half, HD : 2 * HD] = v_ref[...]
    slot = lax.broadcasted_iota(jnp.int32, (SEQ * 64, NCAP), 0)
    wanted = lax.div(slot, 64) * CAPS + lax.rem(slot, CAPS)
    hit = lax.broadcasted_iota(jnp.int32, (SEQ * 64, NCAP), 1) == wanted
    cap_ref[...] = jnp.sum(jnp.where(hit, pos_ref[...], 0), axis=1, keepdims=True)
    own_rows = pl.ds(pl.multiple_of(s * 64, 64), CAPS)
    spots = cap_ref[own_rows, :] - s * TOK
    sel = (lax.broadcasted_iota(jnp.int32, (CAPS, TOK), 1) == spots).astype(F32).astype(BF16)
    for h in range(HEADS):
        picked = jnp.dot(sel, q_ref[:, h * HD : (h + 1) * HD], preferred_element_type=F32)
        cq[s, h * CAPS : (h + 1) * CAPS, :] = picked.astype(BF16)
    pl.semaphore_wait(barrier, SEQ - 1 + 2 * (KVH - 1))

    def cq_copy(j):
        return rcopy(cq.at[s], cq.at[s], cq_s.at[j], cq_r.at[s], (j, k))

    def start_cq(j, carry):
        cq_copy(j).start()
        return carry

    lax.fori_loop(0, s, start_cq, 0)

    def kv_copy(j):
        block = kv.at[pair, half]
        return rcopy(block, block, kv_s.at[j], kv_r.at[pair], pair_dev(pair + j))

    def kz_copy(j):
        block = kv.at[pair - 4, half]
        return rcopy(block, block, kz_s.at[j], kv_r.at[pair - 4], pair_dev(4 + lax.rem(z + j, 4)))

    def kf_copy(p):
        block = kv.at[p, half]
        return rcopy(block, block, kf_s.at[p], kf_r.at[p], sib)

    pl.when(ylo == 0)(lambda: kv_copy(4).start())
    pl.when(z < 3)(lambda: kv_copy(1).start())
    kf_copy(pair).start()

    def w_copy(j, y):
        xx = lax.rem(x + j, XS)
        return rcopy(
            ow_ref.at[whalf, cols(y * XS + xx)], wbuf.at[y, x, whalf], w_s.at[y, j], w_r.at[y, x], x_dev(xx)
        )

    for y in range(2):
        for j in (1, 3):
            w_copy(j, y).start()

    ones = jnp.ones((2 * TOK, HD), BF16)

    def attend(rb, p, own):
        rows = pl.ds(pl.multiple_of(rb * RB, RB), RB)
        keys = kv[p, :, 0:HD]
        vals = jnp.concatenate([kv[p, :, HD : 2 * HD], ones], axis=1)
        if own:
            row_at = lax.broadcasted_iota(jnp.int32, (RB, 2 * TOK), 0) + (core * TOK + rb * RB)
            allowed = lax.broadcasted_iota(jnp.int32, (RB, 2 * TOK), 1) <= row_at
        for h in range(HEADS):
            at = rb * HEADS + h
            query = q_ref[rows, h * HD : (h + 1) * HD]
            sc = lax.dot_general(query, keys, NT, preferred_element_type=F32)
            if own:
                sc = jnp.where(allowed, sc, NEG)
                top = jnp.broadcast_to(jnp.max(sc, axis=1, keepdims=True), (RB, HD))
            else:
                old = m_s[at]
                top = jnp.maximum(old, jnp.max(sc, axis=1, keepdims=True))
            w = jnp.exp2((sc - top[:, 0:1]) * SCALE2).astype(BF16)
            m_s[at] = top
            pv = jnp.dot(w, vals, preferred_element_type=F32)
            if own:
                acc_s[at] = pv
            else:
                f = jnp.exp2((old - top) * SCALE2)
                acc_s[at] = acc_s[at] * jnp.concatenate([f, f], axis=1) + pv

    def attend_two(rh, p, own):
        attend(2 * rh, p, own)
        attend(2 * rh + 1, p, own)

    def attend_all(p):
        def step(rh, carry):
            attend_two(rh, p, False)
            return carry

        lax.fori_loop(0, 2, step, 0)

    def half_arrived(p):
        block = kv.at[p, half]
        rcopy(block, block, kv_s.at[0], kv_r.at[p], sib).wait_recv()
        kf_copy(p).start()

    def sib_arrived(p):
        block = kv.at[p, half]
        rcopy(block, block, kf_s.at[p], kf_r.at[p], sib).wait_recv()

    steps = [
        (ylo == 1, pair - 4),
        (z >= 1, pair - 1),
        (ylo == 1, lax.rem(z + 3, 4)),
        (ylo == 1, lax.rem(z + 1, 4)),
        (ylo == 1, lax.rem(z + 2, 4)),
        (z >= 3, pair - 3),
        (z >= 2, pair - 2),
    ]

    def ready(i):
        needed, p = steps[i]
        pl.when(needed)(lambda: half_arrived(p))

    def run(i):
        needed, p = steps[i]

        def work():
            sib_arrived(p)
            attend_all(p)

        pl.when(needed)(work)

    sib_arrived(pair)
    attend_two(0, pair, True)

    def wait_cq(j, carry):
        rcopy(cq.at[j], cq.at[j], cq_s.at[j], cq_r.at[j], sib).wait_recv()
        return carry

    lax.fori_loop(s + 1, SEQ, wait_cq, 0)
    own_vals = jnp.concatenate([v_ref[...], jnp.ones((TOK, HD), BF16)], axis=1)
    lane = lax.broadcasted_iota(jnp.int32, (TOK, HD), 1)
    for g in range(2):
        queries = cq[g * 8 : (g + 1) * 8].reshape(TOK, HD)
        sc = lax.dot_general(queries, k_ref[...], NT, preferred_element_type=F32)
        key_at = lax.broadcasted_iota(jnp.int32, (TOK, TOK), 1) + s * TOK
        sc = jnp.where(key_at <= cap_ref[g * TOK : (g + 1) * TOK, :], sc, NEG)
        top = jnp.broadcast_to(jnp.max(sc, axis=1, keepdims=True), (TOK, HD))
        w = jnp.exp2((sc - top[:, 0:1]) * SCALE2).astype(BF16)
        pv = jnp.dot(w, own_vals, preferred_element_type=F32)
        total = pv[:, HD:]
        lse = top * SCALE + jnp.log(total)
        hi = lse.astype(BF16).astype(F32)
        mid = (lse - hi).astype(BF16).astype(F32)
        low = lse - hi - mid
        parts = jnp.where(lane < 32, hi, jnp.where(lane < 64, mid, low))
        both = jnp.concatenate([pv[:, :HD] / total, parts], axis=1).astype(BF16)
        cpo[g * 8 : (g + 1) * 8] = both.reshape(8, 64, 2 * HD)

    def cp_copy(j):
        return rcopy(cpo.at[j], cpi.at[s], cp_s.at[j], cp_r.at[s], (j, k))

    def start_cp(j, carry):
        cp_copy(j).start()
        return carry

    lax.fori_loop(s + 1, SEQ, start_cp, 0)

    ready(0)

    def pass_on():
        for j in (1, 3, 2):
            kz_copy(j).start()

    pl.when(ylo == 1)(pass_on)
    for j in (3, 2):
        pl.when(z + j < 4)(lambda j=j: kv_copy(j).start())
    attend_two(1, pair, True)
    ready(1)
    run(0)

    def unpack(block):
        t = block[:, HD:].astype(F32)
        return block[:, :HD].astype(F32), t[:, 0:1] + t[:, 32:33] + t[:, 64:65]

    def combine(j, carry):
        top, total, acc = carry
        rcopy(cpi.at[j], cpi.at[j], cp_s.at[j], cp_r.at[j], sib).wait_recv()
        o, lse = unpack(cpi[j])
        new = jnp.maximum(top, lse)
        a, b = jnp.exp(top - new), jnp.exp(lse - new)
        return new, total * a + b, acc * a + o * b

    own_o, own_lse = unpack(cpo[s])
    top, total, acc = lax.fori_loop(0, s, combine, (own_lse, jnp.ones((64, 1), F32), own_o))
    att = acc / total
    att = jnp.concatenate([att[h * CAPS : (h + 1) * CAPS] for h in range(HEADS)], axis=1).astype(BF16)
    for i in range(KVH):
        local_w[i].wait()
        cro[i] = jnp.dot(att, hw[0:TOK, i * FEAT : (i + 1) * FEAT], preferred_element_type=F32).astype(BF16)

    def cr_copy(j):
        kk = lax.rem(k + j, KVH)
        return rcopy(cro.at[kk], cri.at[k], cr_s.at[j], cr_r.at[k], (s, kk))

    for j in range(1, KVH):
        cr_copy(j).start()
    head_copy.start()

    def v_copy(y):
        xx = lax.rem(x + 2, XS)
        rows = quarter(ylo)
        return rcopy(ow_ref.at[rows, cols(y * XS + xx)], wbuf.at[y, x, rows], v_s.at[y], v_r.at[y], x_dev(xx))

    v_copy(0).start()

    ready(2)
    run(1)

    cap_sum = cro[k].astype(F32) + jnp.dot(sel, hid_ref[...], preferred_element_type=F32)
    for j in range(1, KVH):
        kk = lax.rem(k + j, KVH)
        rcopy(cri.at[kk], cri.at[kk], cr_s.at[0], cr_r.at[kk], sib).wait_recv()
        cap_sum = cap_sum + cri[kk].astype(F32)

    def cap_rows(ss):
        return pl.ds(pl.multiple_of(ss * CAPS, CAPS), CAPS)

    call[k, cap_rows(s), :] = cap_sum.astype(BF16)

    def ck_copy(j):
        block = call.at[k, cap_rows(s)]
        return rcopy(block, block, ck_s.at[j], ck_r.at[k], (s, lax.rem(k + j, KVH)))

    def cy_copy(j):
        block = call.at[k, cap_rows(s)]
        return rcopy(block, block, cy_s.at[j], cy_r.at[k], (2 * y_pair + core, lax.rem(k + j, KVH)))

    for j in range(1, KVH):
        ck_copy(j).start()
    for j in range(KVH):
        cy_copy(j).start()

    v_copy(1).start()

    def wf_copy(j, y):
        block = wbuf.at[y, lax.rem(x + j, XS), whalf]
        return rcopy(block, block, wf_s.at[y, j], wf_r.at[y, j], sib)

    for y in range(2):
        for j in (1, 3):
            xx = lax.rem(x + j, XS)
            block = wbuf.at[y, xx, whalf]
            rcopy(block, block, w_s.at[y, 0], w_r.at[y, xx], sib).wait_recv()
            wf_copy(j, y).start()
    ready(3)
    run(2)

    def cap_block(p, h):
        return call.at[4 * h : 4 * h + 4, cap_rows(2 * p + core)]

    def cs_copy(h, j, p):
        block = cap_block(p, h)
        peer = ylo * 4 + lax.rem(z + j, 4)
        return rcopy(block, block, cs_s.at[h, lax.div(p, 4) * 4 + j], cs_r.at[h, p], pair_dev(peer))

    def cf_copy(h, p):
        block = cap_block(p, h)
        return rcopy(block, block, cf_s.at[h, p], cf_r.at[h, p], sib)

    def spread():
        for j in range(1, KVH):
            kk = lax.rem(k + j, KVH)
            block = call.at[kk, cap_rows(s)]
            rcopy(block, block, ck_s.at[0], ck_r.at[kk], sib).wait_recv()
        for kk in range(KVH):
            block = call.at[kk, cap_rows(2 * y_pair + core)]
            rcopy(block, block, ck_s.at[0], cy_r.at[kk], sib).wait_recv()
        for h in range(2):
            for j in (1, 3, 2):
                for p in (pair, y_pair):
                    cs_copy(h, j, p).start()
            for p in (pair, y_pair):
                cf_copy(h, p).start()

    def cap_arrived(h, p):
        block = cap_block(p, h)
        rcopy(block, block, cs_s.at[h, 0], cs_r.at[h, p], sib).wait_recv()
        cf_copy(h, p).start()

    def a_copy(rb, j):
        block = abuf.at[rb, x]
        return rcopy(block, block, a_s.at[rb, j], a_r.at[rb, x], x_dev(lax.rem(x + j, XS)))

    def finish(rh):
        for i in (4, 5, 6):
            needed, p = steps[i]

            def work():
                if rh == 0:
                    sib_arrived(p)
                attend_two(rh, p, False)

            pl.when(needed)(work)
        for rb in (2 * rh, 2 * rh + 1):
            for h in range(HEADS):
                done = acc_s[rb * HEADS + h]
                abuf[rb, x, :, h * HD : (h + 1) * HD] = (done[:, :HD] / done[:, HD:]).astype(BF16)
            for j in (1, 3, 2):
                a_copy(rb, j).start()

    def y_copy(rb):
        return rcopy(psend.at[rb], precv.at[rb], y_s.at[rb], y_r.at[rb], y_dev)

    def project(rb):
        for j in range(1, XS):
            xx = lax.rem(x + j, XS)
            block = abuf.at[rb, xx]
            rcopy(block, block, a_s.at[rb, 0], a_r.at[rb, xx], sib).wait_recv()

        def product(y):
            parts = [jnp.dot(abuf[rb, xx], wbuf[y, xx], preferred_element_type=F32) for xx in range(XS)]
            return (parts[0] + parts[1]) + (parts[2] + parts[3])

        psend[rb] = product(other_y).astype(BF16)
        y_copy(rb).start()
        lacc[rb] = product(yhi) + hid_ref[rb * RB : (rb + 1) * RB, :].astype(F32)

    x_two = lax.rem(x + 2, XS)

    def vf_copy(y, yy):
        block = wbuf.at[y, x_two, quarter(yy)]
        return rcopy(block, block, vf_s.at[y, yy], vf_r.at[y, yy], sib)

    def vy_copy(y):
        block = wbuf.at[y, x_two, quarter(ylo)]
        return rcopy(block, block, vy_s.at[y], vy_r.at[y], pair_dev(y_pair))

    def v_arrived(y):
        block = wbuf.at[y, x_two, quarter(ylo)]
        rcopy(block, block, v_s.at[0], v_r.at[y], sib).wait_recv()
        vy_copy(y).start()
        vf_copy(y, ylo).start()

    def w_arrived():
        for c in own_w:
            c.wait()
        for y in range(2):
            block = wbuf.at[y, x_two, quarter(1 - ylo)]
            rcopy(block, block, v_s.at[0], vy_r.at[y], sib).wait_recv()
            vf_copy(y, 1 - ylo).start()
        for y in range(2):
            for j in (1, 3):
                block = wbuf.at[y, lax.rem(x + j, XS), whalf]
                rcopy(block, block, wf_s.at[y, 0], wf_r.at[y, j], sib).wait_recv()
            for yy in range(2):
                block = wbuf.at[y, x_two, quarter(yy)]
                rcopy(block, block, v_s.at[0], vf_r.at[y, yy], sib).wait_recv()

    spread()
    v_arrived(0)
    ready(4)
    run(3)
    ready(5)
    ready(6)
    finish(0)
    v_arrived(1)
    finish(1)
    w_arrived()
    project(0)
    project(1)

    def scale(h, p):
        block = cap_block(p, h)
        rcopy(block, block, cf_s.at[h, p], cf_r.at[h, p], sib).wait_recv()
        rows = pl.ds(pl.multiple_of(p * 32, 32), 32)
        wide = [call[kk, rows, :].astype(F32) for kk in range(4 * h, 4 * h + 4)]
        squares = functools.reduce(lambda a, b: a + b, [t * t for t in wide])
        part = jnp.sum(squares, axis=1, keepdims=True)
        ssq[rows, :] = part if h == 0 else ssq[rows, :] + part
        for kk in range(4):
            at = 4 * h + kk
            gain = gain_ref[:, at * FEAT : (at + 1) * FEAT]
            ncap[at, rows, :] = (wide[kk] * gain).astype(BF16)

    def take(h):
        last = pair
        for j in (1, 5, 3, 7, 2, 6):
            p = lax.rem(ylo + j // 4, 2) * 4 + lax.rem(z + j, 4)
            cap_arrived(h, p)
            scale(h, last)
            last = p
        scale(h, y_pair)
        scale(h, last)

    def half_logits(h):
        parts = [
            lax.dot_general(hw[:, kk * FEAT : (kk + 1) * FEAT], ncap[kk], NT, preferred_element_type=F32)
            for kk in range(4 * h, 4 * h + 4)
        ]
        return (parts[0] + parts[1]) + (parts[2] + parts[3])

    def final(rb):
        rcopy(psend.at[rb], precv.at[rb], y_s.at[rb], y_r.at[rb], sib).wait_recv()
        out_ref[rb * RB : (rb + 1) * RB, :] = (lacc[rb] + precv[rb].astype(F32)).astype(BF16)

    take(0)
    head_copy.wait()
    logit[...] = half_logits(0)
    project(2)
    take(1)
    square = (NCAP, NCAP)
    diagonal = lax.broadcasted_iota(jnp.int32, square, 0) == lax.broadcasted_iota(jnp.int32, square, 1)
    mean = jnp.sum(jnp.where(diagonal, ssq[...], 0.0), axis=0, keepdims=True) * (1.0 / (KVH * FEAT))
    lt = (logit[...] + half_logits(1)) * lax.rsqrt(mean + 1e-06)
    ids = lax.broadcasted_iota(jnp.int32, (VOC, NCAP), 0) + (s * KVH + k) * VOC
    top = jnp.max(lt, axis=0, keepdims=True)
    st1[k, 0:1, :] = top
    st1[k, 1:2, :] = jnp.sum(jnp.exp(lt - top), axis=0, keepdims=True)
    st1[k, 2:3, :] = jnp.sum(jnp.where(ids == tgt_ref[...], lt, 0.0), axis=0, keepdims=True)

    def s1_copy(j):
        return rcopy(st1.at[k], st1.at[k], s1_s.at[j], s1_r.at[k], (s, lax.rem(k + j, KVH)))

    def s2_copy(j):
        return rcopy(st2.at[s], st2.at[s], s2_s.at[j], s2_r.at[s], (lax.rem(s + j, SEQ), k))

    def merge(blocks):
        top = jnp.max(blocks[:, 0, :], axis=0, keepdims=True)
        total = jnp.sum(blocks[:, 1, :] * jnp.exp(blocks[:, 0, :] - top), axis=0, keepdims=True)
        return top, total, jnp.sum(blocks[:, 2, :], axis=0, keepdims=True)

    for j in range(1, KVH):
        s1_copy(j).start()
    project(3)
    for j in range(1, KVH):
        kk = lax.rem(k + j, KVH)
        rcopy(st1.at[kk], st1.at[kk], s1_s.at[0], s1_r.at[kk], sib).wait_recv()
    top, total, target = merge(st1[...])
    st2[s, 0:1, :] = top
    st2[s, 1:2, :] = total
    st2[s, 2:3, :] = target
    for j in range(1, SEQ):
        s2_copy(j).start()
    for rb in range(NRB):
        final(rb)
    for j in range(1, SEQ):
        ss = lax.rem(s + j, SEQ)
        rcopy(st2.at[ss], st2.at[ss], s2_s.at[0], s2_r.at[ss], sib).wait_recv()
    top, total, target = merge(st2[...])
    lp_ref[...] = target - (top + jnp.log(total))

    def wait_cq_sent(j, carry):
        cq_copy(j).wait_send()
        return carry

    def wait_cp_sent(j, carry):
        cp_copy(j).wait_send()
        return carry

    def wait_kf_sent(p, carry):
        kf_copy(p).wait_send()
        return carry

    lax.fori_loop(0, s, wait_cq_sent, 0)
    lax.fori_loop(s + 1, SEQ, wait_cp_sent, 0)
    lax.fori_loop(0, pair + 1, wait_kf_sent, 0)
    pl.when(ylo == 0)(lambda: kv_copy(4).wait_send())
    for j in range(1, 4):
        pl.when(z + j < 4)(lambda j=j: kv_copy(j).wait_send())
        pl.when(ylo == 1)(lambda j=j: kz_copy(j).wait_send())
    for h in range(2):
        for j in range(1, 4):
            for p in (pair, y_pair):
                cs_copy(h, j, p).wait_send()
        for p in range(PAIRS):
            cf_copy(h, p).wait_send()
    for y in range(2):
        for j in (1, 3):
            w_copy(j, y).wait_send()
            wf_copy(j, y).wait_send()
        v_copy(y).wait_send()
        vy_copy(y).wait_send()
        for yy in range(2):
            vf_copy(y, yy).wait_send()
    for rb in range(NRB):
        for j in range(1, XS):
            a_copy(rb, j).wait_send()
        y_copy(rb).wait_send()
    cy_copy(0).wait_send()
    for j in range(1, KVH):
        cr_copy(j).wait_send()
        ck_copy(j).wait_send()
        cy_copy(j).wait_send()
        s1_copy(j).wait_send()
    for j in range(1, SEQ):
        s2_copy(j).wait_send()


def body(hidden_in, queries, keys, values, out_weight, norm_gain, head_weight, caption_pos, targets):
    vmem = pl.BlockSpec(memory_space=pltpu.VMEM)
    hbm = pl.BlockSpec(memory_space=pl.ANY)
    dma = lambda *shape: pltpu.SemaphoreType.DMA(shape)
    layer_out, log_probs = pl.pallas_call(
        kernel,
        name="score_captions",
        out_shape=(
            jax.ShapeDtypeStruct((TOK, FEAT), BF16),
            jax.ShapeDtypeStruct((1, NCAP), F32),
        ),
        in_specs=[vmem, vmem, vmem, vmem, hbm, vmem, hbm, vmem, vmem],
        out_specs=(vmem, vmem),
        scratch_shapes=[
            pltpu.VMEM((PAIRS, 2 * TOK, 2 * HD), BF16),
            pltpu.VMEM((NRB * HEADS, RB, HD), F32),
            pltpu.VMEM((NRB * HEADS, RB, 2 * HD), F32),
            pltpu.VMEM((2, XS, TOK, FEAT), BF16),
            pltpu.VMEM((VOC, KVH * FEAT), BF16),
            pltpu.VMEM((KVH, NCAP, FEAT), BF16),
            pltpu.VMEM((KVH, NCAP, FEAT), BF16),
            pltpu.VMEM((NRB, XS, RB, HEADS * HD), BF16),
            pltpu.VMEM((NRB, RB, FEAT), BF16),
            pltpu.VMEM((NRB, RB, FEAT), BF16),
            pltpu.VMEM((NRB, RB, FEAT), F32),
            pltpu.VMEM((SEQ * 64, 1), jnp.int32),
            pltpu.VMEM((SEQ, 64, HD), BF16),
            pltpu.VMEM((SEQ, 64, 2 * HD), BF16),
            pltpu.VMEM((SEQ, 64, 2 * HD), BF16),
            pltpu.VMEM((KVH, CAPS, FEAT), BF16),
            pltpu.VMEM((KVH, CAPS, FEAT), BF16),
            pltpu.VMEM((NCAP, 1), F32),
            pltpu.VMEM((VOC, NCAP), F32),
            pltpu.VMEM((KVH, 8, NCAP), F32),
            pltpu.VMEM((SEQ, 8, NCAP), F32),
            dma(KVH), dma(2), dma(1),
            dma(PAIRS), dma(PAIRS), dma(PAIRS), dma(PAIRS), dma(XS),
            dma(2, XS), dma(2, XS), dma(2, XS), dma(2, XS),
            dma(2), dma(2), dma(2, 2), dma(2, 2), dma(2), dma(2),
            dma(SEQ), dma(SEQ), dma(SEQ), dma(SEQ),
            dma(KVH), dma(KVH), dma(KVH), dma(KVH), dma(KVH), dma(KVH),
            dma(2, PAIRS), dma(2, PAIRS), dma(2, PAIRS), dma(2, PAIRS),
            dma(NRB, XS), dma(NRB, XS), dma(NRB), dma(NRB),
            dma(KVH), dma(KVH), dma(SEQ), dma(SEQ),
        ],
        compiler_params=pltpu.CompilerParams(
            collective_id=0, has_side_effects=True, vmem_limit_bytes=60 * 1024 * 1024
        ),
    )(
        queries, keys, values, hidden_in, out_weight, norm_gain.reshape(1, KVH * FEAT), head_weight,
        caption_pos.reshape(1, NCAP), targets.reshape(1, NCAP),
    )
    return layer_out, log_probs.reshape(NCAP)


def solution(mesh):
    in_specs = (
        P("seq", "kvh"),
        P("seq", "kvh"),
        P("seq", "kvh"),
        P("seq", "kvh"),
        P("kvh", None),
        P(),
        P(("seq", "kvh"), None),
        P(),
        P(),
    )
    out_specs = (P("seq", "kvh"), P())
    return jax.shard_map(body, mesh=mesh, in_specs=in_specs, out_specs=out_specs, check_vma=False)
```

```python
import functools
import jax
import jax.numpy as jnp
from jax import lax
from jax.experimental import pallas as pl
from jax.experimental.pallas import tpu as pltpu
from jax.sharding import PartitionSpec as P

MESH = pl.DeviceIdType.MESH
F32 = jnp.float32
BF16 = jnp.bfloat16
NT = (((1,), (1,)), ((), ()))
NEG = -1e30
SEQ = 16
KVH = 8
PAIRS = 8
XS = 4
TOK = 512
HD = 128
HEADS = 4
RB = 128
NRB = TOK // RB
CAPS = 16
NCAP = SEQ * CAPS
FEAT = 1024
VOC = 640
SCALE = HD ** (-0.5)
SCALE2 = SCALE * 1.4426950408889634


def rcopy(src, dst, send_sem, recv_sem, device):
    return pltpu.make_async_remote_copy(
        src_ref=src,
        dst_ref=dst,
        send_sem=send_sem,
        recv_sem=recv_sem,
        device_id=device,
        device_id_type=MESH,
    )


def kernel(
    q_hbm, k_hbm, v_hbm, hid_hbm, ow_ref, gain_ref, hw_ref, pos_ref, tgt_ref,
    out_ref, lp_ref,
    q_ref, k_ref, v_ref, hid_ref, in_m, kv, m_s, acc_s, wbuf, hw, call, ncap, abuf, psend, precv, lacc,
    cap_ref, cq, cpo, cpi, cro, cri, ssq, logit, st1, st2,
    wl_m, wo_m, hw_m, kv_s, kv_r, kf_s, kf_r, kz_s, w_s, w_r, wf_s, wf_r,
    v_s, v_r, vf_s, vf_r, vy_s, vy_r,
    cq_s, cq_r, cp_s, cp_r, cr_s, cr_r, ck_s, ck_r, cy_s, cy_r, cs_s, cs_r, cf_s, cf_r,
    a_s, a_r, y_s, y_r, s1_s, s1_r, s2_s, s2_r,
):
    s = lax.axis_index("seq")
    k = lax.axis_index("kvh")
    pair, core = lax.div(s, 2), lax.rem(s, 2)
    ylo, z = lax.div(pair, 4), lax.rem(pair, 4)
    yhi, x = lax.div(k, XS), lax.rem(k, XS)
    other_y = 1 - yhi
    sib = (2 * pair + 1 - core, k)
    y_dev = (s, other_y * XS + x)

    def pair_dev(p):
        return (2 * p + core, k)

    def x_dev(xx):
        return (s, yhi * XS + xx)

    def cols(kk):
        return pl.ds(pl.multiple_of(kk * FEAT, FEAT), FEAT)

    half = pl.ds(pl.multiple_of(core * TOK, TOK), TOK)
    whalf = pl.ds(pl.multiple_of(core * 256, 256), 256)
    y_pair = (1 - ylo) * 4 + z

    def quarter(yy):
        return pl.ds(pl.multiple_of((yy * 2 + core) * 128, 128), 128)


    own_w = [
        pltpu.make_async_copy(ow_ref.at[:, cols(y * XS + x)], wbuf.at[y, x], wo_m.at[y])
        for y in range(2)
    ]
    local_w = [
        pltpu.make_async_copy(ow_ref.at[:, cols(i)], hw.at[0:TOK, cols(i)], wl_m.at[i])
        for i in range(KVH)
    ]
    head_copy = pltpu.make_async_copy(hw_ref, hw, hw_m.at[0])
    barrier = pltpu.get_barrier_semaphore()
    for j in range(1, SEQ):
        pl.semaphore_signal(barrier, inc=1, device_id=(lax.rem(s + j, SEQ), k), device_id_type=MESH)
    for j in range(1, KVH):
        pl.semaphore_signal(barrier, inc=1, device_id=(s, lax.rem(k + j, KVH)), device_id_type=MESH)
    for j in range(1, KVH):
        pl.semaphore_signal(
            barrier, inc=1, device_id=(2 * y_pair + core, lax.rem(k + j, KVH)), device_id_type=MESH
        )
    pairs_in = ((q_hbm, q_ref), (k_hbm, k_ref), (v_hbm, v_ref), (hid_hbm, hid_ref))
    own_in = [pltpu.make_async_copy(a, b, in_m.at[i]) for i, (a, b) in enumerate(pairs_in)]
    for c in own_in:
        c.start()
    slot = lax.broadcasted_iota(jnp.int32, (SEQ * 64, NCAP), 0)
    wanted = lax.div(slot, 64) * CAPS + lax.rem(slot, CAPS)
    hit = lax.broadcasted_iota(jnp.int32, (SEQ * 64, NCAP), 1) == wanted
    cap_ref[...] = jnp.sum(jnp.where(hit, pos_ref[...], 0), axis=1, keepdims=True)
    for c in own_in:
        c.wait()
    kv[pair, half, 0:HD] = k_ref[...]
    kv[pair, half, HD : 2 * HD] = v_ref[...]
    own_rows = pl.ds(pl.multiple_of(s * 64, 64), CAPS)
    spots = cap_ref[own_rows, :] - s * TOK
    sel = (lax.broadcasted_iota(jnp.int32, (CAPS, TOK), 1) == spots).astype(F32).astype(BF16)
    for h in range(HEADS):
        picked = jnp.dot(sel, q_ref[:, h * HD : (h + 1) * HD], preferred_element_type=F32)
        cq[s, h * CAPS : (h + 1) * CAPS, :] = picked.astype(BF16)
    pl.semaphore_wait(barrier, SEQ - 1 + 2 * (KVH - 1))

    def cq_copy(j):
        return rcopy(cq.at[s], cq.at[s], cq_s.at[j], cq_r.at[s], (j, k))

    def start_cq(j, carry):
        cq_copy(j).start()
        return carry

    lax.fori_loop(0, s, start_cq, 0)

    def kv_copy(j):
        block = kv.at[pair, half]
        return rcopy(block, block, kv_s.at[j], kv_r.at[pair], pair_dev(pair + j))

    def kz_copy(j):
        block = kv.at[pair - 4, half]
        return rcopy(block, block, kz_s.at[j], kv_r.at[pair - 4], pair_dev(4 + lax.rem(z + j, 4)))

    def kf_copy(p):
        block = kv.at[p, half]
        return rcopy(block, block, kf_s.at[p], kf_r.at[p], sib)

    pl.when(ylo == 0)(lambda: kv_copy(4).start())
    pl.when(z < 3)(lambda: kv_copy(1).start())
    kf_copy(pair).start()

    def w_copy(j, y):
        xx = lax.rem(x + j, XS)
        return rcopy(
            ow_ref.at[whalf, cols(y * XS + xx)], wbuf.at[y, x, whalf], w_s.at[y, j], w_r.at[y, x], x_dev(xx)
        )

    for y in range(2):
        for j in (1, 3):
            w_copy(j, y).start()

    for c in local_w + own_w:
        c.start()

    ones = jnp.ones((2 * TOK, HD), BF16)

    def attend(rb, p, own):
        rows = pl.ds(pl.multiple_of(rb * RB, RB), RB)
        keys = kv[p, :, 0:HD]
        vals = jnp.concatenate([kv[p, :, HD : 2 * HD], ones], axis=1)
        if own:
            row_at = lax.broadcasted_iota(jnp.int32, (RB, 2 * TOK), 0) + (core * TOK + rb * RB)
            allowed = lax.broadcasted_iota(jnp.int32, (RB, 2 * TOK), 1) <= row_at
        for h in range(HEADS):
            at = rb * HEADS + h
            query = q_ref[rows, h * HD : (h + 1) * HD]
            sc = lax.dot_general(query, keys, NT, preferred_element_type=F32)
            if own:
                sc = jnp.where(allowed, sc, NEG)
                top = jnp.broadcast_to(jnp.max(sc, axis=1, keepdims=True), (RB, HD))
            else:
                old = m_s[at]
                top = jnp.maximum(old, jnp.max(sc, axis=1, keepdims=True))
            w = jnp.exp2((sc - top[:, 0:1]) * SCALE2).astype(BF16)
            m_s[at] = top
            pv = jnp.dot(w, vals, preferred_element_type=F32)
            if own:
                acc_s[at] = pv
            else:
                f = jnp.exp2((old - top) * SCALE2)
                acc_s[at] = acc_s[at] * jnp.concatenate([f, f], axis=1) + pv

    def attend_two(rh, p, own):
        attend(2 * rh, p, own)
        attend(2 * rh + 1, p, own)

    def attend_all(p):
        def step(rh, carry):
            attend_two(rh, p, False)
            return carry

        lax.fori_loop(0, 2, step, 0)

    def half_arrived(p):
        block = kv.at[p, half]
        rcopy(block, block, kv_s.at[0], kv_r.at[p], sib).wait_recv()
        kf_copy(p).start()

    def sib_arrived(p):
        block = kv.at[p, half]
        rcopy(block, block, kf_s.at[p], kf_r.at[p], sib).wait_recv()

    steps = [
        (ylo == 1, pair - 4),
        (z >= 1, pair - 1),
        (ylo == 1, lax.rem(z + 3, 4)),
        (ylo == 1, lax.rem(z + 1, 4)),
        (ylo == 1, lax.rem(z + 2, 4)),
        (z >= 3, pair - 3),
        (z >= 2, pair - 2),
    ]

    def ready(i):
        needed, p = steps[i]
        pl.when(needed)(lambda: half_arrived(p))

    def run(i):
        needed, p = steps[i]

        def work():
            sib_arrived(p)
            attend_all(p)

        pl.when(needed)(work)

    sib_arrived(pair)
    attend_two(0, pair, True)

    def wait_cq(j, carry):
        rcopy(cq.at[j], cq.at[j], cq_s.at[j], cq_r.at[j], sib).wait_recv()
        return carry

    lax.fori_loop(s + 1, SEQ, wait_cq, 0)
    own_vals = jnp.concatenate([v_ref[...], jnp.ones((TOK, HD), BF16)], axis=1)
    lane = lax.broadcasted_iota(jnp.int32, (TOK, HD), 1)
    for g in range(2):
        queries = cq[g * 8 : (g + 1) * 8].reshape(TOK, HD)
        sc = lax.dot_general(queries, k_ref[...], NT, preferred_element_type=F32)
        key_at = lax.broadcasted_iota(jnp.int32, (TOK, TOK), 1) + s * TOK
        sc = jnp.where(key_at <= cap_ref[g * TOK : (g + 1) * TOK, :], sc, NEG)
        top = jnp.broadcast_to(jnp.max(sc, axis=1, keepdims=True), (TOK, HD))
        w = jnp.exp2((sc - top[:, 0:1]) * SCALE2).astype(BF16)
        pv = jnp.dot(w, own_vals, preferred_element_type=F32)
        total = pv[:, HD:]
        lse = top * SCALE + jnp.log(total)
        hi = lse.astype(BF16).astype(F32)
        mid = (lse - hi).astype(BF16).astype(F32)
        low = lse - hi - mid
        parts = jnp.where(lane < 32, hi, jnp.where(lane < 64, mid, low))
        both = jnp.concatenate([pv[:, :HD] / total, parts], axis=1).astype(BF16)
        cpo[g * 8 : (g + 1) * 8] = both.reshape(8, 64, 2 * HD)

    def cp_copy(j):
        return rcopy(cpo.at[j], cpi.at[s], cp_s.at[j], cp_r.at[s], (j, k))

    def start_cp(j, carry):
        cp_copy(j).start()
        return carry

    lax.fori_loop(s + 1, SEQ, start_cp, 0)

    ready(0)

    def pass_on():
        for j in (1, 3, 2):
            kz_copy(j).start()

    pl.when(ylo == 1)(pass_on)
    for j in (3, 2):
        pl.when(z + j < 4)(lambda j=j: kv_copy(j).start())
    attend_two(1, pair, True)
    ready(1)
    run(0)

    def unpack(block):
        t = block[:, HD:].astype(F32)
        return block[:, :HD].astype(F32), t[:, 0:1] + t[:, 32:33] + t[:, 64:65]

    def combine(j, carry):
        top, total, acc = carry
        rcopy(cpi.at[j], cpi.at[j], cp_s.at[j], cp_r.at[j], sib).wait_recv()
        o, lse = unpack(cpi[j])
        new = jnp.maximum(top, lse)
        a, b = jnp.exp(top - new), jnp.exp(lse - new)
        return new, total * a + b, acc * a + o * b

    own_o, own_lse = unpack(cpo[s])
    top, total, acc = lax.fori_loop(0, s, combine, (own_lse, jnp.ones((64, 1), F32), own_o))
    att = acc / total
    att = jnp.concatenate([att[h * CAPS : (h + 1) * CAPS] for h in range(HEADS)], axis=1).astype(BF16)
    for i in range(KVH):
        local_w[i].wait()
        cro[i] = jnp.dot(att, hw[0:TOK, i * FEAT : (i + 1) * FEAT], preferred_element_type=F32).astype(BF16)

    def cr_copy(j):
        kk = lax.rem(k + j, KVH)
        return rcopy(cro.at[kk], cri.at[k], cr_s.at[j], cr_r.at[k], (s, kk))

    for j in range(1, KVH):
        cr_copy(j).start()
    head_copy.start()

    def v_copy(y):
        xx = lax.rem(x + 2, XS)
        rows = quarter(ylo)
        return rcopy(ow_ref.at[rows, cols(y * XS + xx)], wbuf.at[y, x, rows], v_s.at[y], v_r.at[y], x_dev(xx))

    v_copy(0).start()

    ready(2)
    run(1)

    cap_sum = cro[k].astype(F32) + jnp.dot(sel, hid_ref[...], preferred_element_type=F32)
    for j in range(1, KVH):
        kk = lax.rem(k + j, KVH)
        rcopy(cri.at[kk], cri.at[kk], cr_s.at[0], cr_r.at[kk], sib).wait_recv()
        cap_sum = cap_sum + cri[kk].astype(F32)

    def cap_rows(ss):
        return pl.ds(pl.multiple_of(ss * CAPS, CAPS), CAPS)

    call[k, cap_rows(s), :] = cap_sum.astype(BF16)

    def ck_copy(j):
        block = call.at[k, cap_rows(s)]
        return rcopy(block, block, ck_s.at[j], ck_r.at[k], (s, lax.rem(k + j, KVH)))

    def cy_copy(j):
        block = call.at[k, cap_rows(s)]
        return rcopy(block, block, cy_s.at[j], cy_r.at[k], (2 * y_pair + core, lax.rem(k + j, KVH)))

    for j in range(1, KVH):
        ck_copy(j).start()
    for j in range(KVH):
        cy_copy(j).start()

    v_copy(1).start()

    def wf_copy(j, y):
        block = wbuf.at[y, lax.rem(x + j, XS), whalf]
        return rcopy(block, block, wf_s.at[y, j], wf_r.at[y, j], sib)

    for y in range(2):
        for j in (1, 3):
            xx = lax.rem(x + j, XS)
            block = wbuf.at[y, xx, whalf]
            rcopy(block, block, w_s.at[y, 0], w_r.at[y, xx], sib).wait_recv()
            wf_copy(j, y).start()
    ready(3)
    run(2)

    def cap_block(p, h):
        return call.at[4 * h : 4 * h + 4, cap_rows(2 * p + core)]

    def cs_copy(h, j, p):
        block = cap_block(p, h)
        peer = ylo * 4 + lax.rem(z + j, 4)
        return rcopy(block, block, cs_s.at[h, lax.div(p, 4) * 4 + j], cs_r.at[h, p], pair_dev(peer))

    def cf_copy(h, p):
        block = cap_block(p, h)
        return rcopy(block, block, cf_s.at[h, p], cf_r.at[h, p], sib)

    def spread():
        for j in range(1, KVH):
            kk = lax.rem(k + j, KVH)
            block = call.at[kk, cap_rows(s)]
            rcopy(block, block, ck_s.at[0], ck_r.at[kk], sib).wait_recv()
        for kk in range(KVH):
            block = call.at[kk, cap_rows(2 * y_pair + core)]
            rcopy(block, block, ck_s.at[0], cy_r.at[kk], sib).wait_recv()
        for h in range(2):
            for j in (1, 3, 2):
                for p in (pair, y_pair):
                    cs_copy(h, j, p).start()
            for p in (pair, y_pair):
                cf_copy(h, p).start()

    def cap_arrived(h, p):
        block = cap_block(p, h)
        rcopy(block, block, cs_s.at[h, 0], cs_r.at[h, p], sib).wait_recv()
        cf_copy(h, p).start()

    def a_copy(rb, j):
        block = abuf.at[rb, x]
        return rcopy(block, block, a_s.at[rb, j], a_r.at[rb, x], x_dev(lax.rem(x + j, XS)))

    def finish(rh):
        for i in (3, 4, 5, 6):
            needed, p = steps[i]

            def work():
                if rh == 0:
                    sib_arrived(p)
                attend_two(rh, p, False)

            pl.when(needed)(work)
        for rb in (2 * rh, 2 * rh + 1):
            for h in range(HEADS):
                done = acc_s[rb * HEADS + h]
                abuf[rb, x, :, h * HD : (h + 1) * HD] = (done[:, :HD] / done[:, HD:]).astype(BF16)
            for j in (1, 3, 2):
                a_copy(rb, j).start()

    def y_copy(rb):
        return rcopy(psend.at[rb], precv.at[rb], y_s.at[rb], y_r.at[rb], y_dev)

    def project(rb):
        for j in range(1, XS):
            xx = lax.rem(x + j, XS)
            block = abuf.at[rb, xx]
            rcopy(block, block, a_s.at[rb, 0], a_r.at[rb, xx], sib).wait_recv()

        def product(y):
            parts = [jnp.dot(abuf[rb, xx], wbuf[y, xx], preferred_element_type=F32) for xx in range(XS)]
            return (parts[0] + parts[1]) + (parts[2] + parts[3])

        psend[rb] = product(other_y).astype(BF16)
        y_copy(rb).start()
        lacc[rb] = product(yhi) + hid_ref[rb * RB : (rb + 1) * RB, :].astype(F32)

    x_two = lax.rem(x + 2, XS)

    def vf_copy(y, yy):
        block = wbuf.at[y, x_two, quarter(yy)]
        return rcopy(block, block, vf_s.at[y, yy], vf_r.at[y, yy], sib)

    def vy_copy(y):
        block = wbuf.at[y, x_two, quarter(ylo)]
        return rcopy(block, block, vy_s.at[y], vy_r.at[y], pair_dev(y_pair))

    def v_arrived(y):
        block = wbuf.at[y, x_two, quarter(ylo)]
        rcopy(block, block, v_s.at[0], v_r.at[y], sib).wait_recv()
        vy_copy(y).start()
        vf_copy(y, ylo).start()

    def w_arrived():
        for c in own_w:
            c.wait()
        for y in range(2):
            block = wbuf.at[y, x_two, quarter(1 - ylo)]
            rcopy(block, block, v_s.at[0], vy_r.at[y], sib).wait_recv()
            vf_copy(y, 1 - ylo).start()
        for y in range(2):
            for j in (1, 3):
                block = wbuf.at[y, lax.rem(x + j, XS), whalf]
                rcopy(block, block, wf_s.at[y, 0], wf_r.at[y, j], sib).wait_recv()
            for yy in range(2):
                block = wbuf.at[y, x_two, quarter(yy)]
                rcopy(block, block, v_s.at[0], vf_r.at[y, yy], sib).wait_recv()

    spread()
    v_arrived(0)
    ready(4)
    ready(5)
    ready(6)
    finish(0)
    v_arrived(1)
    finish(1)

    def scale(h, p):
        block = cap_block(p, h)
        rcopy(block, block, cf_s.at[h, p], cf_r.at[h, p], sib).wait_recv()
        rows = pl.ds(pl.multiple_of(p * 32, 32), 32)
        wide = [call[kk, rows, :].astype(F32) for kk in range(4 * h, 4 * h + 4)]
        squares = functools.reduce(lambda a, b: a + b, [t * t for t in wide])
        part = jnp.sum(squares, axis=1, keepdims=True)
        ssq[rows, :] = part if h == 0 else ssq[rows, :] + part
        for kk in range(4):
            at = 4 * h + kk
            gain = gain_ref[:, at * FEAT : (at + 1) * FEAT]
            ncap[at, rows, :] = (wide[kk] * gain).astype(BF16)

    def take(h):
        last = pair
        for j in (1, 5, 3, 7, 2, 6):
            p = lax.rem(ylo + j // 4, 2) * 4 + lax.rem(z + j, 4)
            cap_arrived(h, p)
            scale(h, last)
            last = p
        scale(h, y_pair)
        scale(h, last)

    def half_logits(h):
        parts = [
            lax.dot_general(hw[:, kk * FEAT : (kk + 1) * FEAT], ncap[kk], NT, preferred_element_type=F32)
            for kk in range(4 * h, 4 * h + 4)
        ]
        return (parts[0] + parts[1]) + (parts[2] + parts[3])

    def final(rb):
        rcopy(psend.at[rb], precv.at[rb], y_s.at[rb], y_r.at[rb], sib).wait_recv()
        out_ref[rb * RB : (rb + 1) * RB, :] = (lacc[rb] + precv[rb].astype(F32)).astype(BF16)

    take(0)
    w_arrived()
    project(0)
    head_copy.wait()
    logit[...] = half_logits(0)
    project(1)
    project(2)
    take(1)
    square = (NCAP, NCAP)
    diagonal = lax.broadcasted_iota(jnp.int32, square, 0) == lax.broadcasted_iota(jnp.int32, square, 1)
    mean = jnp.sum(jnp.where(diagonal, ssq[...], 0.0), axis=0, keepdims=True) * (1.0 / (KVH * FEAT))
    lt = (logit[...] + half_logits(1)) * lax.rsqrt(mean + 1e-06)
    ids = lax.broadcasted_iota(jnp.int32, (VOC, NCAP), 0) + (s * KVH + k) * VOC
    top = jnp.max(lt, axis=0, keepdims=True)
    st2[s, 0:1, :] = top
    st2[s, 1:2, :] = jnp.sum(jnp.exp(lt - top), axis=0, keepdims=True)
    st2[s, 2:3, :] = jnp.sum(jnp.where(ids == tgt_ref[...], lt, 0.0), axis=0, keepdims=True)

    def s1_copy(j):
        return rcopy(st1.at[k], st1.at[k], s1_s.at[j], s1_r.at[k], (s, lax.rem(k + j, KVH)))

    def s2_copy(j):
        return rcopy(st2.at[s], st2.at[s], s2_s.at[j], s2_r.at[s], (lax.rem(s + j, SEQ), k))

    def merge(blocks):
        top = jnp.max(blocks[:, 0, :], axis=0, keepdims=True)
        total = jnp.sum(blocks[:, 1, :] * jnp.exp(blocks[:, 0, :] - top), axis=0, keepdims=True)
        return top, total, jnp.sum(blocks[:, 2, :], axis=0, keepdims=True)

    for j in range(1, SEQ):
        s2_copy(j).start()
    project(3)
    for j in range(1, SEQ):
        ss = lax.rem(s + j, SEQ)
        rcopy(st2.at[ss], st2.at[ss], s2_s.at[0], s2_r.at[ss], sib).wait_recv()
    top, total, target = merge(st2[...])
    st1[k, 0:1, :] = top
    st1[k, 1:2, :] = total
    st1[k, 2:3, :] = target
    for j in range(1, KVH):
        s1_copy(j).start()
    for rb in range(NRB):
        final(rb)
    for j in range(1, KVH):
        kk = lax.rem(k + j, KVH)
        rcopy(st1.at[kk], st1.at[kk], s1_s.at[0], s1_r.at[kk], sib).wait_recv()
    top, total, target = merge(st1[...])
    lp_ref[...] = target - (top + jnp.log(total))

    def wait_cq_sent(j, carry):
        cq_copy(j).wait_send()
        return carry

    def wait_cp_sent(j, carry):
        cp_copy(j).wait_send()
        return carry

    def wait_kf_sent(p, carry):
        kf_copy(p).wait_send()
        return carry

    lax.fori_loop(0, s, wait_cq_sent, 0)
    lax.fori_loop(s + 1, SEQ, wait_cp_sent, 0)
    lax.fori_loop(0, pair + 1, wait_kf_sent, 0)
    pl.when(ylo == 0)(lambda: kv_copy(4).wait_send())
    for j in range(1, 4):
        pl.when(z + j < 4)(lambda j=j: kv_copy(j).wait_send())
        pl.when(ylo == 1)(lambda j=j: kz_copy(j).wait_send())
    for h in range(2):
        for j in range(1, 4):
            for p in (pair, y_pair):
                cs_copy(h, j, p).wait_send()
        for p in range(PAIRS):
            cf_copy(h, p).wait_send()
    for y in range(2):
        for j in (1, 3):
            w_copy(j, y).wait_send()
            wf_copy(j, y).wait_send()
        v_copy(y).wait_send()
        vy_copy(y).wait_send()
        for yy in range(2):
            vf_copy(y, yy).wait_send()
    for rb in range(NRB):
        for j in range(1, XS):
            a_copy(rb, j).wait_send()
        y_copy(rb).wait_send()
    cy_copy(0).wait_send()
    for j in range(1, KVH):
        cr_copy(j).wait_send()
        ck_copy(j).wait_send()
        cy_copy(j).wait_send()
        s1_copy(j).wait_send()
    for j in range(1, SEQ):
        s2_copy(j).wait_send()


def hand_over(a_ref, b_ref, c_ref, d_ref, held, small, in_sems, out_sems):
    parts = [pl.ds(i * RB, RB) for i in range(NRB)]
    copies = [pltpu.make_async_copy(a_ref.at[r], held.at[r], in_sems.at[i]) for i, r in enumerate(parts)]
    copies.append(pltpu.make_async_copy(b_ref, small, in_sems.at[NRB]))
    onward = [pltpu.make_async_copy(held.at[r], c_ref.at[r], out_sems.at[i]) for i, r in enumerate(parts)]
    onward.append(pltpu.make_async_copy(small, d_ref, out_sems.at[NRB]))
    for c in copies:
        c.start()
    for c, d in zip(copies, onward):
        c.wait()
        d.start()
    for d in onward:
        d.wait()


def body(hidden_in, queries, keys, values, out_weight, norm_gain, head_weight, caption_pos, targets):
    vmem = pl.BlockSpec(memory_space=pltpu.VMEM)
    hbm = pl.BlockSpec(memory_space=pl.ANY)
    dma = lambda *shape: pltpu.SemaphoreType.DMA(shape)
    layer_out, log_probs = pl.pallas_call(
        kernel,
        name="score_captions",
        out_shape=(
            jax.ShapeDtypeStruct((TOK, FEAT), BF16),
            jax.ShapeDtypeStruct((1, NCAP), F32),
        ),
        in_specs=[hbm, hbm, hbm, hbm, hbm, vmem, hbm, vmem, vmem],
        out_specs=(vmem, vmem),
        scratch_shapes=[
            pltpu.VMEM((TOK, HEADS * HD), BF16),
            pltpu.VMEM((TOK, HD), BF16),
            pltpu.VMEM((TOK, HD), BF16),
            pltpu.VMEM((TOK, FEAT), BF16),
            dma(4),
            pltpu.VMEM((PAIRS, 2 * TOK, 2 * HD), BF16),
            pltpu.VMEM((NRB * HEADS, RB, HD), F32),
            pltpu.VMEM((NRB * HEADS, RB, 2 * HD), F32),
            pltpu.VMEM((2, XS, TOK, FEAT), BF16),
            pltpu.VMEM((VOC, KVH * FEAT), BF16),
            pltpu.VMEM((KVH, NCAP, FEAT), BF16),
            pltpu.VMEM((KVH, NCAP, FEAT), BF16),
            pltpu.VMEM((NRB, XS, RB, HEADS * HD), BF16),
            pltpu.VMEM((NRB, RB, FEAT), BF16),
            pltpu.VMEM((NRB, RB, FEAT), BF16),
            pltpu.VMEM((NRB, RB, FEAT), F32),
            pltpu.VMEM((SEQ * 64, 1), jnp.int32),
            pltpu.VMEM((SEQ, 64, HD), BF16),
            pltpu.VMEM((SEQ, 64, 2 * HD), BF16),
            pltpu.VMEM((SEQ, 64, 2 * HD), BF16),
            pltpu.VMEM((KVH, CAPS, FEAT), BF16),
            pltpu.VMEM((KVH, CAPS, FEAT), BF16),
            pltpu.VMEM((NCAP, 1), F32),
            pltpu.VMEM((VOC, NCAP), F32),
            pltpu.VMEM((KVH, 8, NCAP), F32),
            pltpu.VMEM((SEQ, 8, NCAP), F32),
            dma(KVH), dma(2), dma(1),
            dma(PAIRS), dma(PAIRS), dma(PAIRS), dma(PAIRS), dma(XS),
            dma(2, XS), dma(2, XS), dma(2, XS), dma(2, XS),
            dma(2), dma(2), dma(2, 2), dma(2, 2), dma(2), dma(2),
            dma(SEQ), dma(SEQ), dma(SEQ), dma(SEQ),
            dma(KVH), dma(KVH), dma(KVH), dma(KVH), dma(KVH), dma(KVH),
            dma(2, PAIRS), dma(2, PAIRS), dma(2, PAIRS), dma(2, PAIRS),
            dma(NRB, XS), dma(NRB, XS), dma(NRB), dma(NRB),
            dma(KVH), dma(KVH), dma(SEQ), dma(SEQ),
        ],
        compiler_params=pltpu.CompilerParams(
            collective_id=0, has_side_effects=True, vmem_limit_bytes=60 * 1024 * 1024
        ),
    )(
        queries, keys, values, hidden_in, out_weight, norm_gain.reshape(1, KVH * FEAT), head_weight,
        caption_pos.reshape(1, NCAP), targets.reshape(1, NCAP),
    )
    layer_out, log_probs = pl.pallas_call(
        hand_over,
        name="hand_over",
        out_shape=(
            jax.ShapeDtypeStruct((TOK, FEAT), BF16),
            jax.ShapeDtypeStruct((1, NCAP), F32),
        ),
        in_specs=[hbm, hbm],
        out_specs=(hbm, hbm),
        scratch_shapes=[
            pltpu.VMEM((TOK, FEAT), BF16),
            pltpu.VMEM((1, NCAP), F32),
            dma(NRB + 1),
            dma(NRB + 1),
        ],
    )(layer_out, log_probs)
    return layer_out, log_probs.reshape(NCAP)


def solution(mesh):
    in_specs = (
        P("seq", "kvh"),
        P("seq", "kvh"),
        P("seq", "kvh"),
        P("seq", "kvh"),
        P("kvh", None),
        P(),
        P(("seq", "kvh"), None),
        P(),
        P(),
    )
    out_specs = (P("seq", "kvh"), P())
    return jax.shard_map(body, mesh=mesh, in_specs=in_specs, out_specs=out_specs, check_vma=False)
```

```python
import functools
import jax
import jax.numpy as jnp
from jax import lax
from jax.experimental import pallas as pl
from jax.experimental.pallas import tpu as pltpu
from jax.sharding import PartitionSpec as P

MESH = pl.DeviceIdType.MESH
F32 = jnp.float32
BF16 = jnp.bfloat16
NT = (((1,), (1,)), ((), ()))
NEG = -1e30
SEQ = 16
KVH = 8
PAIRS = 8
XS = 4
TOK = 512
HD = 128
HEADS = 4
RB = 128
NRB = TOK // RB
CAPS = 16
NCAP = SEQ * CAPS
FEAT = 1024
VOC = 640
SCALE = HD ** (-0.5)
SCALE2 = SCALE * 1.4426950408889634


def rcopy(src, dst, send_sem, recv_sem, device):
    return pltpu.make_async_remote_copy(
        src_ref=src,
        dst_ref=dst,
        send_sem=send_sem,
        recv_sem=recv_sem,
        device_id=device,
        device_id_type=MESH,
    )


def kernel(
    q_ref, k_ref, v_ref, hid_ref, ow_ref, gain_ref, hw_ref, pos_ref, tgt_ref,
    out_ref, lp_ref,
    kv, m_s, acc_s, wbuf, hw, call, ncap, abuf, psend, precv, lacc,
    cap_ref, cq, cpo, cpi, cro, cri, ssq, logit, st1, st2,
    wl_m, wo_m, hw_m, kv_s, kv_r, kf_s, kf_r, kz_s, w_s, w_r, wf_s, wf_r,
    v_s, v_r, vf_s, vf_r, vy_s, vy_r,
    cq_s, cq_r, cp_s, cp_r, cr_s, cr_r, ck_s, ck_r, cy_s, cy_r, cs_s, cs_r, cf_s, cf_r,
    a_s, a_r, y_s, y_r, s1_s, s1_r, s2_s, s2_r,
):
    s = lax.axis_index("seq")
    k = lax.axis_index("kvh")
    pair, core = lax.div(s, 2), lax.rem(s, 2)
    ylo, z = lax.div(pair, 4), lax.rem(pair, 4)
    yhi, x = lax.div(k, XS), lax.rem(k, XS)
    other_y = 1 - yhi
    sib = (2 * pair + 1 - core, k)
    y_dev = (s, other_y * XS + x)

    def pair_dev(p):
        return (2 * p + core, k)

    def x_dev(xx):
        return (s, yhi * XS + xx)

    def cols(kk):
        return pl.ds(pl.multiple_of(kk * FEAT, FEAT), FEAT)

    half = pl.ds(pl.multiple_of(core * TOK, TOK), TOK)
    whalf = pl.ds(pl.multiple_of(core * 256, 256), 256)
    y_pair = (1 - ylo) * 4 + z

    def quarter(yy):
        return pl.ds(pl.multiple_of((yy * 2 + core) * 128, 128), 128)


    own_w = [
        pltpu.make_async_copy(ow_ref.at[:, cols(y * XS + x)], wbuf.at[y, x], wo_m.at[y])
        for y in range(2)
    ]
    local_w = [
        pltpu.make_async_copy(ow_ref.at[:, cols(i)], hw.at[0:TOK, cols(i)], wl_m.at[i])
        for i in range(KVH)
    ]
    head_copy = pltpu.make_async_copy(hw_ref, hw, hw_m.at[0])
    barrier = pltpu.get_barrier_semaphore()
    for j in range(1, SEQ):
        pl.semaphore_signal(barrier, inc=1, device_id=(lax.rem(s + j, SEQ), k), device_id_type=MESH)
    for j in range(1, KVH):
        pl.semaphore_signal(barrier, inc=1, device_id=(s, lax.rem(k + j, KVH)), device_id_type=MESH)
    for j in range(1, KVH):
        pl.semaphore_signal(
            barrier, inc=1, device_id=(2 * y_pair + core, lax.rem(k + j, KVH)), device_id_type=MESH
        )
    for c in local_w + own_w:
        c.start()
    kv[pair, half, 0:HD] = k_ref[...]
    kv[pair, half, HD : 2 * HD] = v_ref[...]
    slot = lax.broadcasted_iota(jnp.int32, (SEQ * 64, NCAP), 0)
    wanted = lax.div(slot, 64) * CAPS + lax.rem(slot, CAPS)
    hit = lax.broadcasted_iota(jnp.int32, (SEQ * 64, NCAP), 1) == wanted
    cap_ref[...] = jnp.sum(jnp.where(hit, pos_ref[...], 0), axis=1, keepdims=True)
    own_rows = pl.ds(pl.multiple_of(s * 64, 64), CAPS)
    spots = cap_ref[own_rows, :] - s * TOK
    sel = (lax.broadcasted_iota(jnp.int32, (CAPS, TOK), 1) == spots).astype(F32).astype(BF16)
    for h in range(HEADS):
        picked = jnp.dot(sel, q_ref[:, h * HD : (h + 1) * HD], preferred_element_type=F32)
        cq[s, h * CAPS : (h + 1) * CAPS, :] = picked.astype(BF16)
    pl.semaphore_wait(barrier, SEQ - 1 + 2 * (KVH - 1))

    def cq_copy(j):
        return rcopy(cq.at[s], cq.at[s], cq_s.at[j], cq_r.at[s], (j, k))

    def start_cq(j, carry):
        cq_copy(j).start()
        return carry

    lax.fori_loop(0, s, start_cq, 0)

    def kv_copy(j):
        block = kv.at[pair, half]
        return rcopy(block, block, kv_s.at[j], kv_r.at[pair], pair_dev(pair + j))

    def kz_copy(j):
        block = kv.at[pair - 4, half]
        return rcopy(block, block, kz_s.at[j], kv_r.at[pair - 4], pair_dev(4 + lax.rem(z + j, 4)))

    def kf_copy(p):
        block = kv.at[p, half]
        return rcopy(block, block, kf_s.at[p], kf_r.at[p], sib)

    pl.when(ylo == 0)(lambda: kv_copy(4).start())
    pl.when(z < 3)(lambda: kv_copy(1).start())
    kf_copy(pair).start()

    def w_copy(j, y):
        xx = lax.rem(x + j, XS)
        return rcopy(
            ow_ref.at[whalf, cols(y * XS + xx)], wbuf.at[y, x, whalf], w_s.at[y, j], w_r.at[y, x], x_dev(xx)
        )

    for y in range(2):
        for j in (1, 3):
            w_copy(j, y).start()

    ones = jnp.ones((2 * TOK, HD), BF16)

    def attend(rb, p, own):
        rows = pl.ds(pl.multiple_of(rb * RB, RB), RB)
        keys = kv[p, :, 0:HD]
        vals = jnp.concatenate([kv[p, :, HD : 2 * HD], ones], axis=1)
        if own:
            row_at = lax.broadcasted_iota(jnp.int32, (RB, 2 * TOK), 0) + (core * TOK + rb * RB)
            allowed = lax.broadcasted_iota(jnp.int32, (RB, 2 * TOK), 1) <= row_at
        for h in range(HEADS):
            at = rb * HEADS + h
            query = q_ref[rows, h * HD : (h + 1) * HD]
            sc = lax.dot_general(query, keys, NT, preferred_element_type=F32)
            if own:
                sc = jnp.where(allowed, sc, NEG)
                top = jnp.broadcast_to(jnp.max(sc, axis=1, keepdims=True), (RB, HD))
            else:
                old = m_s[at]
                top = jnp.maximum(old, jnp.max(sc, axis=1, keepdims=True))
            w = jnp.exp2((sc - top[:, 0:1]) * SCALE2).astype(BF16)
            m_s[at] = top
            pv = jnp.dot(w, vals, preferred_element_type=F32)
            if own:
                acc_s[at] = pv
            else:
                f = jnp.exp2((old - top) * SCALE2)
                acc_s[at] = acc_s[at] * jnp.concatenate([f, f], axis=1) + pv

    def attend_two(rh, p, own):
        attend(2 * rh, p, own)
        attend(2 * rh + 1, p, own)

    def attend_all(p):
        def step(rh, carry):
            attend_two(rh, p, False)
            return carry

        lax.fori_loop(0, 2, step, 0)

    def half_arrived(p):
        block = kv.at[p, half]
        rcopy(block, block, kv_s.at[0], kv_r.at[p], sib).wait_recv()
        kf_copy(p).start()

    def sib_arrived(p):
        block = kv.at[p, half]
        rcopy(block, block, kf_s.at[p], kf_r.at[p], sib).wait_recv()

    steps = [
        (ylo == 1, pair - 4),
        (z >= 1, pair - 1),
        (ylo == 1, lax.rem(z + 3, 4)),
        (ylo == 1, lax.rem(z + 1, 4)),
        (ylo == 1, lax.rem(z + 2, 4)),
        (z >= 3, pair - 3),
        (z >= 2, pair - 2),
    ]

    def ready(i):
        needed, p = steps[i]
        pl.when(needed)(lambda: half_arrived(p))

    def run(i):
        needed, p = steps[i]

        def work():
            sib_arrived(p)
            attend_all(p)

        pl.when(needed)(work)

    sib_arrived(pair)
    attend_two(0, pair, True)

    def wait_cq(j, carry):
        rcopy(cq.at[j], cq.at[j], cq_s.at[j], cq_r.at[j], sib).wait_recv()
        return carry

    lax.fori_loop(s + 1, SEQ, wait_cq, 0)
    own_vals = jnp.concatenate([v_ref[...], jnp.ones((TOK, HD), BF16)], axis=1)
    lane = lax.broadcasted_iota(jnp.int32, (TOK, HD), 1)
    for g in range(2):
        queries = cq[g * 8 : (g + 1) * 8].reshape(TOK, HD)
        sc = lax.dot_general(queries, k_ref[...], NT, preferred_element_type=F32)
        key_at = lax.broadcasted_iota(jnp.int32, (TOK, TOK), 1) + s * TOK
        sc = jnp.where(key_at <= cap_ref[g * TOK : (g + 1) * TOK, :], sc, NEG)
        top = jnp.broadcast_to(jnp.max(sc, axis=1, keepdims=True), (TOK, HD))
        w = jnp.exp2((sc - top[:, 0:1]) * SCALE2).astype(BF16)
        pv = jnp.dot(w, own_vals, preferred_element_type=F32)
        total = pv[:, HD:]
        lse = top * SCALE + jnp.log(total)
        hi = lse.astype(BF16).astype(F32)
        mid = (lse - hi).astype(BF16).astype(F32)
        low = lse - hi - mid
        parts = jnp.where(lane < 32, hi, jnp.where(lane < 64, mid, low))
        both = jnp.concatenate([pv[:, :HD] / total, parts], axis=1).astype(BF16)
        cpo[g * 8 : (g + 1) * 8] = both.reshape(8, 64, 2 * HD)

    def cp_copy(j):
        return rcopy(cpo.at[j], cpi.at[s], cp_s.at[j], cp_r.at[s], (j, k))

    def start_cp(j, carry):
        cp_copy(j).start()
        return carry

    lax.fori_loop(s + 1, SEQ, start_cp, 0)

    ready(0)

    def pass_on():
        for j in (1, 3, 2):
            kz_copy(j).start()

    pl.when(ylo == 1)(pass_on)
    for j in (3, 2):
        pl.when(z + j < 4)(lambda j=j: kv_copy(j).start())
    attend_two(1, pair, True)
    ready(1)
    run(0)

    def unpack(block):
        t = block[:, HD:].astype(F32)
        return block[:, :HD].astype(F32), t[:, 0:1] + t[:, 32:33] + t[:, 64:65]

    def combine(j, carry):
        top, total, acc = carry
        rcopy(cpi.at[j], cpi.at[j], cp_s.at[j], cp_r.at[j], sib).wait_recv()
        o, lse = unpack(cpi[j])
        new = jnp.maximum(top, lse)
        a, b = jnp.exp(top - new), jnp.exp(lse - new)
        return new, total * a + b, acc * a + o * b

    own_o, own_lse = unpack(cpo[s])
    top, total, acc = lax.fori_loop(0, s, combine, (own_lse, jnp.ones((64, 1), F32), own_o))
    att = acc / total
    att = jnp.concatenate([att[h * CAPS : (h + 1) * CAPS] for h in range(HEADS)], axis=1).astype(BF16)
    for i in range(KVH):
        local_w[i].wait()
        cro[i] = jnp.dot(att, hw[0:TOK, i * FEAT : (i + 1) * FEAT], preferred_element_type=F32).astype(BF16)

    def cr_copy(j):
        kk = lax.rem(k + j, KVH)
        return rcopy(cro.at[kk], cri.at[k], cr_s.at[j], cr_r.at[k], (s, kk))

    for j in range(1, KVH):
        cr_copy(j).start()
    head_copy.start()

    def v_copy(y):
        xx = lax.rem(x + 2, XS)
        rows = quarter(ylo)
        return rcopy(ow_ref.at[rows, cols(y * XS + xx)], wbuf.at[y, x, rows], v_s.at[y], v_r.at[y], x_dev(xx))

    v_copy(0).start()

    ready(2)
    run(1)

    cap_sum = cro[k].astype(F32) + jnp.dot(sel, hid_ref[...], preferred_element_type=F32)
    for j in range(1, KVH):
        kk = lax.rem(k + j, KVH)
        rcopy(cri.at[kk], cri.at[kk], cr_s.at[0], cr_r.at[kk], sib).wait_recv()
        cap_sum = cap_sum + cri[kk].astype(F32)

    def cap_rows(ss):
        return pl.ds(pl.multiple_of(ss * CAPS, CAPS), CAPS)

    call[k, cap_rows(s), :] = cap_sum.astype(BF16)

    def ck_copy(j):
        block = call.at[k, cap_rows(s)]
        return rcopy(block, block, ck_s.at[j], ck_r.at[k], (s, lax.rem(k + j, KVH)))

    def cy_copy(j):
        block = call.at[k, cap_rows(s)]
        return rcopy(block, block, cy_s.at[j], cy_r.at[k], (2 * y_pair + core, lax.rem(k + j, KVH)))

    for j in range(1, KVH):
        ck_copy(j).start()
    for j in range(KVH):
        cy_copy(j).start()

    v_copy(1).start()

    def wf_copy(j, y):
        block = wbuf.at[y, lax.rem(x + j, XS), whalf]
        return rcopy(block, block, wf_s.at[y, j], wf_r.at[y, j], sib)

    for y in range(2):
        for j in (1, 3):
            xx = lax.rem(x + j, XS)
            block = wbuf.at[y, xx, whalf]
            rcopy(block, block, w_s.at[y, 0], w_r.at[y, xx], sib).wait_recv()
            wf_copy(j, y).start()
    ready(3)
    run(2)

    def cap_block(p, h):
        return call.at[4 * h : 4 * h + 4, cap_rows(2 * p + core)]

    def cs_copy(h, j, p):
        block = cap_block(p, h)
        peer = ylo * 4 + lax.rem(z + j, 4)
        return rcopy(block, block, cs_s.at[h, lax.div(p, 4) * 4 + j], cs_r.at[h, p], pair_dev(peer))

    def cf_copy(h, p):
        block = cap_block(p, h)
        return rcopy(block, block, cf_s.at[h, p], cf_r.at[h, p], sib)

    def spread():
        for j in range(1, KVH):
            kk = lax.rem(k + j, KVH)
            block = call.at[kk, cap_rows(s)]
            rcopy(block, block, ck_s.at[0], ck_r.at[kk], sib).wait_recv()
        for kk in range(KVH):
            block = call.at[kk, cap_rows(2 * y_pair + core)]
            rcopy(block, block, ck_s.at[0], cy_r.at[kk], sib).wait_recv()
        for h in range(2):
            for j in (1, 3, 2):
                for p in (pair, y_pair):
                    cs_copy(h, j, p).start()
            for p in (pair, y_pair):
                cf_copy(h, p).start()

    def cap_arrived(h, p):
        block = cap_block(p, h)
        rcopy(block, block, cs_s.at[h, 0], cs_r.at[h, p], sib).wait_recv()
        cf_copy(h, p).start()

    def a_copy(rb, j):
        block = abuf.at[rb, x]
        return rcopy(block, block, a_s.at[rb, j], a_r.at[rb, x], x_dev(lax.rem(x + j, XS)))

    def finish(rh):
        for i in (3, 4, 5, 6):
            needed, p = steps[i]

            def work():
                if rh == 0:
                    sib_arrived(p)
                attend_two(rh, p, False)

            pl.when(needed)(work)
        for rb in (2 * rh, 2 * rh + 1):
            for h in range(HEADS):
                done = acc_s[rb * HEADS + h]
                abuf[rb, x, :, h * HD : (h + 1) * HD] = (done[:, :HD] / done[:, HD:]).astype(BF16)
            for j in (1, 3, 2):
                a_copy(rb, j).start()

    def y_copy(rb):
        return rcopy(psend.at[rb], precv.at[rb], y_s.at[rb], y_r.at[rb], y_dev)

    def project(rb):
        for j in range(1, XS):
            xx = lax.rem(x + j, XS)
            block = abuf.at[rb, xx]
            rcopy(block, block, a_s.at[rb, 0], a_r.at[rb, xx], sib).wait_recv()

        def product(y):
            parts = [jnp.dot(abuf[rb, xx], wbuf[y, xx], preferred_element_type=F32) for xx in range(XS)]
            return (parts[0] + parts[1]) + (parts[2] + parts[3])

        psend[rb] = product(other_y).astype(BF16)
        y_copy(rb).start()
        lacc[rb] = product(yhi) + hid_ref[rb * RB : (rb + 1) * RB, :].astype(F32)

    x_two = lax.rem(x + 2, XS)

    def vf_copy(y, yy):
        block = wbuf.at[y, x_two, quarter(yy)]
        return rcopy(block, block, vf_s.at[y, yy], vf_r.at[y, yy], sib)

    def vy_copy(y):
        block = wbuf.at[y, x_two, quarter(ylo)]
        return rcopy(block, block, vy_s.at[y], vy_r.at[y], pair_dev(y_pair))

    def v_arrived(y):
        block = wbuf.at[y, x_two, quarter(ylo)]
        rcopy(block, block, v_s.at[0], v_r.at[y], sib).wait_recv()
        vy_copy(y).start()
        vf_copy(y, ylo).start()

    def w_arrived():
        for c in own_w:
            c.wait()
        for y in range(2):
            block = wbuf.at[y, x_two, quarter(1 - ylo)]
            rcopy(block, block, v_s.at[0], vy_r.at[y], sib).wait_recv()
            vf_copy(y, 1 - ylo).start()
        for y in range(2):
            for j in (1, 3):
                block = wbuf.at[y, lax.rem(x + j, XS), whalf]
                rcopy(block, block, wf_s.at[y, 0], wf_r.at[y, j], sib).wait_recv()
            for yy in range(2):
                block = wbuf.at[y, x_two, quarter(yy)]
                rcopy(block, block, v_s.at[0], vf_r.at[y, yy], sib).wait_recv()

    spread()
    v_arrived(0)
    ready(4)
    ready(5)
    ready(6)
    finish(0)
    v_arrived(1)
    finish(1)

    def scale(h, p):
        block = cap_block(p, h)
        rcopy(block, block, cf_s.at[h, p], cf_r.at[h, p], sib).wait_recv()
        rows = pl.ds(pl.multiple_of(p * 32, 32), 32)
        wide = [call[kk, rows, :].astype(F32) for kk in range(4 * h, 4 * h + 4)]
        squares = functools.reduce(lambda a, b: a + b, [t * t for t in wide])
        part = jnp.sum(squares, axis=1, keepdims=True)
        ssq[rows, :] = part if h == 0 else ssq[rows, :] + part
        for kk in range(4):
            at = 4 * h + kk
            gain = gain_ref[:, at * FEAT : (at + 1) * FEAT]
            ncap[at, rows, :] = (wide[kk] * gain).astype(BF16)

    def take(h):
        last = pair
        for j in (1, 5, 3, 7, 2, 6):
            p = lax.rem(ylo + j // 4, 2) * 4 + lax.rem(z + j, 4)
            cap_arrived(h, p)
            scale(h, last)
            last = p
        scale(h, y_pair)
        scale(h, last)

    def half_logits(h):
        parts = [
            lax.dot_general(hw[:, kk * FEAT : (kk + 1) * FEAT], ncap[kk], NT, preferred_element_type=F32)
            for kk in range(4 * h, 4 * h + 4)
        ]
        return (parts[0] + parts[1]) + (parts[2] + parts[3])

    def final(rb):
        rcopy(psend.at[rb], precv.at[rb], y_s.at[rb], y_r.at[rb], sib).wait_recv()
        out_ref[rb * RB : (rb + 1) * RB, :] = (lacc[rb] + precv[rb].astype(F32)).astype(BF16)

    take(0)
    w_arrived()
    project(0)
    head_copy.wait()
    logit[...] = half_logits(0)
    project(1)
    project(2)
    take(1)
    square = (NCAP, NCAP)
    diagonal = lax.broadcasted_iota(jnp.int32, square, 0) == lax.broadcasted_iota(jnp.int32, square, 1)
    mean = jnp.sum(jnp.where(diagonal, ssq[...], 0.0), axis=0, keepdims=True) * (1.0 / (KVH * FEAT))
    lt = (logit[...] + half_logits(1)) * lax.rsqrt(mean + 1e-06)
    ids = lax.broadcasted_iota(jnp.int32, (VOC, NCAP), 0) + (s * KVH + k) * VOC
    top = jnp.max(lt, axis=0, keepdims=True)
    st2[s, 0:1, :] = top
    st2[s, 1:2, :] = jnp.sum(jnp.exp(lt - top), axis=0, keepdims=True)
    st2[s, 2:3, :] = jnp.sum(jnp.where(ids == tgt_ref[...], lt, 0.0), axis=0, keepdims=True)

    def s1_copy(j):
        return rcopy(st1.at[k], st1.at[k], s1_s.at[j], s1_r.at[k], (s, lax.rem(k + j, KVH)))

    def s2_copy(j):
        return rcopy(st2.at[s], st2.at[s], s2_s.at[j], s2_r.at[s], (lax.rem(s + j, SEQ), k))

    def merge(blocks):
        top = jnp.max(blocks[:, 0, :], axis=0, keepdims=True)
        total = jnp.sum(blocks[:, 1, :] * jnp.exp(blocks[:, 0, :] - top), axis=0, keepdims=True)
        return top, total, jnp.sum(blocks[:, 2, :], axis=0, keepdims=True)

    for j in range(1, SEQ):
        s2_copy(j).start()
    project(3)
    for j in range(1, SEQ):
        ss = lax.rem(s + j, SEQ)
        rcopy(st2.at[ss], st2.at[ss], s2_s.at[0], s2_r.at[ss], sib).wait_recv()
    top, total, target = merge(st2[...])
    st1[k, 0:1, :] = top
    st1[k, 1:2, :] = total
    st1[k, 2:3, :] = target
    for j in range(1, KVH):
        s1_copy(j).start()
    for rb in range(NRB):
        final(rb)
    for j in range(1, KVH):
        kk = lax.rem(k + j, KVH)
        rcopy(st1.at[kk], st1.at[kk], s1_s.at[0], s1_r.at[kk], sib).wait_recv()
    top, total, target = merge(st1[...])
    lp_ref[...] = target - (top + jnp.log(total))

    def wait_cq_sent(j, carry):
        cq_copy(j).wait_send()
        return carry

    def wait_cp_sent(j, carry):
        cp_copy(j).wait_send()
        return carry

    def wait_kf_sent(p, carry):
        kf_copy(p).wait_send()
        return carry

    lax.fori_loop(0, s, wait_cq_sent, 0)
    lax.fori_loop(s + 1, SEQ, wait_cp_sent, 0)
    lax.fori_loop(0, pair + 1, wait_kf_sent, 0)
    pl.when(ylo == 0)(lambda: kv_copy(4).wait_send())
    for j in range(1, 4):
        pl.when(z + j < 4)(lambda j=j: kv_copy(j).wait_send())
        pl.when(ylo == 1)(lambda j=j: kz_copy(j).wait_send())
    for h in range(2):
        for j in range(1, 4):
            for p in (pair, y_pair):
                cs_copy(h, j, p).wait_send()
        for p in range(PAIRS):
            cf_copy(h, p).wait_send()
    for y in range(2):
        for j in (1, 3):
            w_copy(j, y).wait_send()
            wf_copy(j, y).wait_send()
        v_copy(y).wait_send()
        vy_copy(y).wait_send()
        for yy in range(2):
            vf_copy(y, yy).wait_send()
    for rb in range(NRB):
        for j in range(1, XS):
            a_copy(rb, j).wait_send()
        y_copy(rb).wait_send()
    cy_copy(0).wait_send()
    for j in range(1, KVH):
        cr_copy(j).wait_send()
        ck_copy(j).wait_send()
        cy_copy(j).wait_send()
        s1_copy(j).wait_send()
    for j in range(1, SEQ):
        s2_copy(j).wait_send()


def body(hidden_in, queries, keys, values, out_weight, norm_gain, head_weight, caption_pos, targets):
    vmem = pl.BlockSpec(memory_space=pltpu.VMEM)
    hbm = pl.BlockSpec(memory_space=pl.ANY)
    dma = lambda *shape: pltpu.SemaphoreType.DMA(shape)
    layer_out, log_probs = pl.pallas_call(
        kernel,
        name="score_captions",
        out_shape=(
            jax.ShapeDtypeStruct((TOK, FEAT), BF16),
            jax.ShapeDtypeStruct((1, NCAP), F32),
        ),
        in_specs=[vmem, vmem, vmem, vmem, hbm, vmem, hbm, vmem, vmem],
        out_specs=(vmem, vmem),
        scratch_shapes=[
            pltpu.VMEM((PAIRS, 2 * TOK, 2 * HD), BF16),
            pltpu.VMEM((NRB * HEADS, RB, HD), F32),
            pltpu.VMEM((NRB * HEADS, RB, 2 * HD), F32),
            pltpu.VMEM((2, XS, TOK, FEAT), BF16),
            pltpu.VMEM((VOC, KVH * FEAT), BF16),
            pltpu.VMEM((KVH, NCAP, FEAT), BF16),
            pltpu.VMEM((KVH, NCAP, FEAT), BF16),
            pltpu.VMEM((NRB, XS, RB, HEADS * HD), BF16),
            pltpu.VMEM((NRB, RB, FEAT), BF16),
            pltpu.VMEM((NRB, RB, FEAT), BF16),
            pltpu.VMEM((NRB, RB, FEAT), F32),
            pltpu.VMEM((SEQ * 64, 1), jnp.int32),
            pltpu.VMEM((SEQ, 64, HD), BF16),
            pltpu.VMEM((SEQ, 64, 2 * HD), BF16),
            pltpu.VMEM((SEQ, 64, 2 * HD), BF16),
            pltpu.VMEM((KVH, CAPS, FEAT), BF16),
            pltpu.VMEM((KVH, CAPS, FEAT), BF16),
            pltpu.VMEM((NCAP, 1), F32),
            pltpu.VMEM((VOC, NCAP), F32),
            pltpu.VMEM((KVH, 8, NCAP), F32),
            pltpu.VMEM((SEQ, 8, NCAP), F32),
            dma(KVH), dma(2), dma(1),
            dma(PAIRS), dma(PAIRS), dma(PAIRS), dma(PAIRS), dma(XS),
            dma(2, XS), dma(2, XS), dma(2, XS), dma(2, XS),
            dma(2), dma(2), dma(2, 2), dma(2, 2), dma(2), dma(2),
            dma(SEQ), dma(SEQ), dma(SEQ), dma(SEQ),
            dma(KVH), dma(KVH), dma(KVH), dma(KVH), dma(KVH), dma(KVH),
            dma(2, PAIRS), dma(2, PAIRS), dma(2, PAIRS), dma(2, PAIRS),
            dma(NRB, XS), dma(NRB, XS), dma(NRB), dma(NRB),
            dma(KVH), dma(KVH), dma(SEQ), dma(SEQ),
        ],
        compiler_params=pltpu.CompilerParams(
            collective_id=0, has_side_effects=True, vmem_limit_bytes=60 * 1024 * 1024
        ),
    )(
        queries, keys, values, hidden_in, out_weight, norm_gain.reshape(1, KVH * FEAT), head_weight,
        caption_pos.reshape(1, NCAP), targets.reshape(1, NCAP),
    )
    return layer_out, log_probs.reshape(NCAP)


def solution(mesh):
    in_specs = (
        P("seq", "kvh"),
        P("seq", "kvh"),
        P("seq", "kvh"),
        P("seq", "kvh"),
        P("kvh", None),
        P(),
        P(("seq", "kvh"), None),
        P(),
        P(),
    )
    out_specs = (P("seq", "kvh"), P())
    return jax.shard_map(body, mesh=mesh, in_specs=in_specs, out_specs=out_specs, check_vma=False)
```
